128 devices in a mesh: segment: 16 (over z_lo, x, core), dp: 8 (over y, z_hi).
Axes of the slice: x: 4, y: 4, z: 4 (z_hi: 2, z_lo: 2; z = z_hi * 2 + z_lo), core: 2. Of those that a mesh axis runs over, the one named last changes fastest.
Arguments:
- stream_in: bfloat16 [1024, 8192], P('dp'), may hold values from -6 to 6
- sec_gain: float32 [16, 8192], P('segment'), may hold values from 0.25 to 1.75
- sec_mix: float32 [16, 8192], P('segment'), may hold values from -3 to 3
- fc_weight: bfloat16 [3, 8192, 8192], P(None, 'dp', 'segment'), may hold values from -0.0390625 to 0.0390625
- decay: float32 [8192], P('segment'), may hold values from 0.2 to 0.97
- lengths: int32 [8, 8], P('dp'), may hold values from 1 to 16
- ttt_mask: int32 [7, 1024], P(None, 'dp'), may hold values 0 or 1
Outputs:
- step_loss: float32 [8, 7], P('dp')
- fc_grad: float32 [3, 8192, 8192], P(None, 'dp', 'segment')
The draws below stay inside these ranges and needn't reach their ends.
All inputs are finite; a program needn't handle non-finite values. No bound on the sum of `ttt_mask` on one device may be relied on, other than what follows from the above.
Results may differ from the reference program's by a relative error of at most 0.0047.
Values may be sent and summed in bfloat16 or wider, within the bound.
A program may use at most 128 MiB of HBM per device.

```python
import math
import jax
import jax.numpy as jnp
from jax import lax

D = 8192
MB = 16
NMB = 8
STEPS = 7
SECTIONS = 16
TOK = 128
ALL_TOK = 1024
N_DP = 8


def touch_ends(result, own_key, low, high):
    shape = result.shape
    index_at = [jax.random.randint(jax.random.fold_in(own_key, axis), (), 0, shape[axis]) for axis in range(len(shape))]
    result = result.at[tuple(index_at)].set(low)
    longest = shape.index(max(shape))
    index_at[longest] = (index_at[longest] + 1) % shape[longest]
    return result.at[tuple(index_at)].set(high)


def shard_levels(own_key, extent, cuts, smallest, largest):
    factor_of = 1.0
    for dim, parts in cuts:
        draws = jax.random.uniform(jax.random.fold_in(jax.random.fold_in(own_key, 6), dim), (parts,), jnp.float32, smallest / len(cuts), largest / len(cuts))
        factor_of = factor_of * jnp.repeat(jnp.exp(draws), extent[dim] // parts).reshape((-1,) + (1,) * (len(extent) - 1 - dim))
    return factor_of


def centred(rng, shape, scale, reach, shards=(), kind=jnp.bfloat16):
    drawn = jax.random.normal(rng, shape, jnp.float32) * scale
    if len(shards) > 0:
        drawn = shard_levels(rng, shape, shards, -0.22, 0.18) * drawn
    return jnp.clip(drawn, min=-reach, max=reach).astype(kind)


def setup_inputs(seed: int = 0) -> dict:
    arg_keys = jax.random.split(jax.random.key(seed), 8)
    stream_in = centred(arg_keys[0], (ALL_TOK, D), 1.0, 6.0, ((0, 8),))
    sec_gain = jnp.clip(1.0 + 0.15 * jax.random.normal(arg_keys[1], (SECTIONS, D), jnp.float32), 0.25, 1.75)
    sec_mix = centred(arg_keys[2], (SECTIONS, D), 0.5, 3.0, ((0, 16),), jnp.float32)
    fc_weight = centred(arg_keys[3], (3, D, D), (3 * D) ** -0.5, 0.0390625, ((1, 8), (2, 16)))
    decay = jnp.clip(jnp.exp(math.log(0.97) - 1.57897872 * jax.random.uniform(arg_keys[4], (D,), jnp.float32) ** shard_levels(arg_keys[4], (D,), ((0, 16),), -0.2, 0.2)), 0.2, 0.97)
    lengths = touch_ends(jax.random.randint(arg_keys[5], (N_DP, NMB), 1, MB + 1), jax.random.fold_in(arg_keys[5], 1), 1, MB).astype(jnp.int32)
    ttt_mask = touch_ends((jax.random.randint(arg_keys[6], (STEPS, ALL_TOK), 0, 4) < 3).astype(jnp.int32), jax.random.fold_in(arg_keys[6], 1), 0, 1)
    return {"stream_in": stream_in, "sec_gain": sec_gain, "sec_mix": sec_mix, "fc_weight": fc_weight, "decay": decay, "lengths": lengths, "ttt_mask": ttt_mask}


def section_step(hidden, gain, mix):
    values = hidden.astype(jnp.float32)
    scale = jnp.sqrt(lax.optimization_barrier(jnp.mean(values * values, axis=-1, keepdims=True)) + 1e-05)
    return (values + mix * jax.nn.silu(gain * values / scale)).astype(jnp.bfloat16)

def unroll_losses(joined, upper, decay, tok_len, masks, width):
    count_tok = joined.shape[0]
    columns = joined.shape[1]
    position = jnp.arange(count_tok, dtype=jnp.int32) % MB
    keep_prev = (position >= 1).astype(jnp.float32)[:, None]
    state = joined
    losses = []
    for step in range(1, STEPS + 1):
        before = jnp.concatenate([jnp.zeros((1, columns), jnp.float32), state[:-1]], 0) * keep_prev
        state = joined + decay[None, :] * masks[step - 1].astype(jnp.float32)[:, None] * before
        target = jnp.concatenate([upper[step:], jnp.zeros((step, columns), jnp.float32)], 0)
        weight = (position + step < tok_len).astype(jnp.float32)
        count = jnp.sum(weight)
        differ = state - target
        total = jnp.sum(weight[:, None] * differ * differ)
        losses.append(total / (width * jnp.maximum(count, 1.0)))
    return jnp.stack(losses)

def reference(stream_in, sec_gain, sec_mix, fc_weight, decay, lengths, ttt_mask):
    hidden = stream_in
    low_tap = hidden
    mid_tap = hidden
    high_tap = hidden
    for section in range(SECTIONS):
        hidden = section_step(hidden, sec_gain[section], sec_mix[section])
        if section == 0:
            low_tap = hidden
        if section == SECTIONS // 2:
            mid_tap = hidden
        if section == SECTIONS - 1:
            high_tap = hidden
    joined = jnp.dot(low_tap, fc_weight[0], preferred_element_type=jnp.float32)
    joined = joined + jnp.dot(mid_tap, fc_weight[1], preferred_element_type=jnp.float32)
    joined = joined + jnp.dot(high_tap, fc_weight[2], preferred_element_type=jnp.float32)
    upper = high_tap.astype(jnp.float32).reshape(N_DP, TOK, D)
    tok_len = jnp.repeat(lengths, MB, axis=1)
    masks = jnp.transpose(ttt_mask.reshape(STEPS, N_DP, TOK), (1, 0, 2))

    def objective(joined_all):
        per_rep = jax.vmap(lambda fr, ur, lr, mr: unroll_losses(fr, ur, decay, lr, mr, D))(joined_all.reshape(N_DP, TOK, D), upper, tok_len, masks)
        return (jnp.sum(per_rep), per_rep)
    total, vjp_fn, step_loss = jax.vjp(objective, joined, has_aux=True)
    joined_grad = vjp_fn(jnp.ones_like(total))[0]
    grad_rows = joined_grad.astype(jnp.bfloat16)
    fc_grad = jnp.stack([jnp.dot(low_tap.T, grad_rows, preferred_element_type=jnp.float32), jnp.dot(mid_tap.T, grad_rows, preferred_element_type=jnp.float32), jnp.dot(high_tap.T, grad_rows, preferred_element_type=jnp.float32)])
    return (step_loss, fc_grad)
```

```python
import jax
import jax.numpy as jnp
from jax import lax
from jax.sharding import PartitionSpec as P

D = 8192
MB = 16
NMB = 8
STEPS = 7
SECTIONS = 16


def section_step(hidden, gain, mix):
    values = hidden.astype(jnp.float32)
    scale = jnp.sqrt(jnp.mean(values * values, axis=-1, keepdims=True) + 1e-05)
    return (values + mix * jax.nn.silu(gain * values / scale)).astype(jnp.bfloat16)


def unroll_losses(joined, upper, decay, tok_len, masks, width):
    count_tok = joined.shape[0]
    columns = joined.shape[1]
    position = jnp.arange(count_tok, dtype=jnp.int32) % MB
    keep_prev = (position >= 1).astype(jnp.float32)[:, None]
    state = joined
    losses = []
    for step in range(1, STEPS + 1):
        before = jnp.concatenate([jnp.zeros((1, columns), jnp.float32), state[:-1]], 0) * keep_prev
        state = joined + decay[None, :] * masks[step - 1].astype(jnp.float32)[:, None] * before
        target = jnp.concatenate([upper[step:], jnp.zeros((step, columns), jnp.float32)], 0)
        weight = (position + step < tok_len).astype(jnp.float32)
        count = jnp.sum(weight)
        differ = state - target
        total = jnp.sum(weight[:, None] * differ * differ)
        losses.append(total / (width * jnp.maximum(count, 1.0)))
    return jnp.stack(losses)


def local(stream_in, sec_gain, sec_mix, fc_weight, decay, lengths, ttt_mask):
    seg = lax.axis_index("segment")
    n_seg = lax.axis_size("segment")
    tok = stream_in.shape[0]
    own = tok // n_seg
    params = lax.all_gather(jnp.concatenate([sec_gain, sec_mix]), "segment", axis=0, tiled=False)
    hidden = lax.dynamic_slice_in_dim(stream_in, seg * own, own, 0)
    taps = []
    for s in range(SECTIONS):
        hidden = section_step(hidden, params[s, 0], params[s, 1])
        if s in (0, SECTIONS // 2, SECTIONS - 1):
            taps.append(hidden)
    taps = jnp.stack(taps)
    mine = lax.all_to_all(taps, "dp", split_axis=2, concat_axis=1, tiled=True)
    n_dp = lax.axis_size("dp")
    out_cols = fc_weight.shape[2]
    features = lax.all_gather(mine, "segment", axis=0, tiled=False)
    features = features.reshape(n_seg, 3, n_dp, own, fc_weight.shape[1])
    features = features.transpose(1, 2, 0, 3, 4).reshape(3, n_dp * tok, fc_weight.shape[1])
    upper = lax.all_to_all(
        taps[2].reshape(own, n_seg, out_cols), "segment", split_axis=1, concat_axis=0, tiled=True
    ).reshape(tok, out_cols).astype(jnp.float32)
    joined = lax.psum_scatter(
        jnp.einsum("bcr,brd->cd", features, fc_weight, preferred_element_type=jnp.float32),
        "dp",
        scatter_dimension=0,
        tiled=True,
    )
    tok_len = jnp.repeat(lengths[0], MB)

    def local_objective(joined_local):
        partial_losses = unroll_losses(joined_local, upper, decay, tok_len, ttt_mask, D)
        return (jnp.sum(partial_losses), partial_losses)

    total, vjp_fn, partial_losses = jax.vjp(local_objective, joined, has_aux=True)
    joined_grad = vjp_fn(jnp.ones_like(total))[0]
    step_loss = lax.psum(partial_losses, "segment")
    grad_rows = joined_grad.astype(jnp.bfloat16)
    rows = lax.all_gather(grad_rows, "dp", axis=0, tiled=True)
    fc_grad = jnp.einsum("bcr,cd->brd", features, rows, preferred_element_type=jnp.float32)
    return (step_loss[None, :], fc_grad)


def solution(mesh):
    in_specs = (
        P("dp", None),
        P("segment", None),
        P("segment", None),
        P(None, "dp", "segment"),
        P("segment"),
        P("dp", None),
        P(None, "dp"),
    )
    out_specs = (P("dp", None), P(None, "dp", "segment"))
    return jax.shard_map(local, mesh=mesh, in_specs=in_specs, out_specs=out_specs, check_vma=False)
```

```python
import functools

import jax
import jax.numpy as jnp
from jax import lax
from jax.experimental import pallas as pl
from jax.experimental.pallas import tpu as pltpu
from jax.sharding import PartitionSpec as P

D = 8192
MB = 16
NMB = 8
STEPS = 7
SECTIONS = 16
TAPS = (0, SECTIONS // 2, SECTIONS - 1)
TOK = 128
SEG = 16
DP = 8
IN = D // DP
OUT = D // SEG
OWN = TOK // SEG
F32 = jnp.float32
BF16 = jnp.bfloat16
MESH = pl.DeviceIdType.MESH


def at(segment, dp):
    return {"segment": segment, "dp": dp}


def advance(h, half_gain, mix, inv):
    u = (h * half_gain) * inv
    return (h + (mix * u) * (1.0 + jnp.tanh(u))).astype(BF16)


def run_sections(h, inv_cols, gain_of, mix_of):
    rows = h.shape[0]
    taps = []
    for sec in range(SECTIONS):
        gain = jnp.concatenate([gain_of(sec)] * (rows // 8), 0)
        mix = jnp.concatenate([mix_of(sec)] * (rows // 8), 0)
        out = advance(h, gain, mix, inv_cols[:, sec:sec + 1])
        if sec in TAPS:
            taps.append(out)
        h = out.astype(F32)
    return taps


def kernel(stream, gain, mix, weight, decay, lengths, mask, loss_out, grad_out,
           gain_all, mix_all, gain_b, mix_b, gain_u, mix_u, rows16, hx, h0, tile, sc1, packed, sc2, inv_own, inv_j,
           w, feat, feat_t, stage, parts, own_part, up_in, upper, mask_t, mask_pad, left, loss_acc, loss_tile,
           loss_all, rows_own, rows_all, grad,
           in_sem, g_send, m_send, g_recv, m_recv, gf_send, mf_send, h_send, h_recv, r1_send, r1_recv, r2_send,
           r2_recv, f_send, f_recv, p_send, p_recv, q_send, q_recv, l_send, l_recv, o_sem):
    s = lax.axis_index("segment")
    d = lax.axis_index("dp")
    c = lax.rem(s, 2)
    sib = s + 1 - 2 * c
    home = lax.rem(d, 2) == c
    seg_peers = [lax.rem(s + i, SEG) for i in range(1, SEG)]
    dp_peers = [lax.rem(d + i, DP) for i in range(1, DP)]
    remote = functools.partial(pltpu.make_async_remote_copy, device_id_type=MESH)

    w_copies = [
        pltpu.make_async_copy(weight.at[i], w.at[pl.ds(i * IN, IN)], in_sem.at[i]) for i in range(3)
    ]
    row0 = pl.multiple_of((s // 2) * 16, 16)
    rows_copy = pltpu.make_async_copy(stream.at[pl.ds(row0, 16)], rows16, in_sem.at[3])
    up_copy = pltpu.make_async_copy(
        stream.at[:, pl.ds(pl.multiple_of(s * OUT, OUT), OUT)], up_in, in_sem.at[4]
    )
    rows_copy.start()
    gain_copy = pltpu.make_async_copy(gain, gain_all.at[s], g_recv.at[s])
    mix_copy = pltpu.make_async_copy(mix, mix_all.at[s], m_recv.at[s])
    gain_copy.start()
    mix_copy.start()

    barrier = pltpu.get_barrier_semaphore()
    for peer in seg_peers:
        pl.semaphore_signal(barrier, inc=1, device_id=at(peer, d), device_id_type=MESH)
    for peer in dp_peers:
        pl.semaphore_signal(barrier, inc=1, device_id=at(s, peer), device_id_type=MESH)
    pl.semaphore_wait(barrier, SEG - 1 + DP - 1)

    first = [sib] + [lax.rem(s + 2 * i, SEG) for i in range(1, SEG // 2)]
    g_sends = []
    for i, peer in enumerate(first):
        for src, dst, snd, rcv in ((gain, gain_all, g_send, g_recv), (mix, mix_all, m_send, m_recv)):
            copy = remote(src, dst.at[s], snd.at[i], rcv.at[s], device_id=at(peer, d))
            copy.start()
            g_sends.append(copy)

    def h_copy(i):
        peer = lax.rem(d + i, DP)
        return remote(
            stream.at[:, pl.ds(pl.multiple_of(peer * IN, IN), IN)], h0.at[d // 2],
            h_send.at[i], h_recv.at[d // 2], device_id=at(s, peer),
        )

    @pl.when(home)
    def _():
        for i in range(1, DP):
            h_copy(i).start()
        pltpu.make_async_copy(
            stream.at[:, pl.ds(pl.multiple_of(d * IN, IN), IN)], h0.at[d // 2], h_recv.at[d // 2]
        ).start()

    up_copy.start()
    for copy in w_copies:
        copy.start()

    token = lax.broadcasted_iota(jnp.int32, (TOK, 128), 0)
    pos = token & (MB - 1)
    micro = lax.shift_right_logical(token, 4)
    tok_len = jnp.zeros((TOK, 128), jnp.int32)
    for m in range(NMB):
        tok_len = jnp.where(micro == m, lengths[0, m], tok_len)
    left[...] = tok_len - pos
    mask_pad[...] = jnp.zeros_like(mask_pad)
    mask_pad[0:STEPS, :] = mask[...].astype(F32)
    mask_t[...] = jnp.where(pos >= 1, mask_pad[...].T, 0.0)
    loss_acc[...] = jnp.zeros_like(loss_acc)

    def wait_param(slot):
        remote(gain, gain_all.at[slot], g_send.at[0], g_recv.at[slot], device_id=at(sib, d)).wait_recv()
        remote(mix, mix_all.at[slot], m_send.at[0], m_recv.at[slot], device_id=at(sib, d)).wait_recv()

    for i in range(1, SEG // 2):
        slot = lax.rem(s + 2 * i, SEG)
        wait_param(slot)
        for dst, snd, rcv in ((gain_all, gf_send, g_recv), (mix_all, mf_send, m_recv)):
            copy = remote(dst.at[slot], dst.at[slot], snd.at[i], rcv.at[slot], device_id=at(sib, d))
            copy.start()
            g_sends.append(copy)
    gain_copy.wait()
    mix_copy.wait()
    wait_param(sib)
    for i in range(1, SEG // 2):
        wait_param(lax.rem(sib + 2 * i, SEG))

    rows_copy.wait()
    hx[...] = rows16[...].astype(F32)
    half = pl.ds(pl.multiple_of(c * OWN, OWN), OWN)
    lane = lax.broadcasted_iota(jnp.int32, (OWN, 128), 1)

    def inverse(h):
        return lax.rsqrt(jnp.sum(h * h, axis=1, keepdims=True) * (1.0 / D) + 1e-05)

    def scale_step(sec, carry):
        inv, acc = carry
        acc = jnp.where(lane == sec, inv, acc)
        h = advance(hx[half, :], 0.5 * gain_all[sec], mix_all[sec], inv).astype(F32)
        hx[half, :] = h
        return inverse(h), acc

    inv, acc = lax.fori_loop(
        0, SECTIONS - 1, scale_step, (inverse(hx[half, :]), jnp.zeros((OWN, 128), F32))
    )
    tile[...] = jnp.where(lane == SECTIONS - 1, inv, acc)
    sc1[s] = tile[...]
    r1_sends = []
    for i, peer in enumerate(seg_peers):
        copy = remote(tile, sc1.at[s], r1_send.at[i], r1_recv.at[s], device_id=at(peer, d))
        copy.start()
        r1_sends.append(copy)

    def spread(sec, _):
        g = 0.5 * gain_all[sec]
        m = mix_all[sec]
        gain_b[sec] = jnp.broadcast_to(0.5 * gain_all[sec, :, pl.ds(pl.multiple_of(d * IN, IN), IN)], (8, IN))
        mix_b[sec] = jnp.broadcast_to(mix_all[sec, :, pl.ds(pl.multiple_of(d * IN, IN), IN)], (8, IN))
        gain_u[sec] = jnp.broadcast_to(0.5 * gain_all[sec, :, pl.ds(pl.multiple_of(s * OUT, OUT), OUT)], (8, OUT))
        mix_u[sec] = jnp.broadcast_to(mix_all[sec, :, pl.ds(pl.multiple_of(s * OUT, OUT), OUT)], (8, OUT))
        return 0

    lax.fori_loop(0, SECTIONS, spread, 0)
    for i, peer in enumerate(seg_peers):
        remote(tile, sc1.at[peer], r1_send.at[i], r1_recv.at[peer], device_id=at(peer, d)).wait_recv()
    inv_own[...] = sc1[...].reshape(TOK, 128)
    packed[...] = inv_own[...].T[0:SECTIONS, :]

    def r2_copy(i):
        peer = lax.rem(d + i, DP)
        return remote(packed, sc2.at[d], r2_send.at[i], r2_recv.at[d], device_id=at(s, peer))

    @pl.when(home)
    def _():
        for i in range(1, DP):
            r2_copy(i).start()
        sc2[d] = packed[...]

    for copy in w_copies:
        copy.wait()

    def replica_of(first_home, n):
        base = jnp.where(first_home, d, d + 1)
        return lax.rem(base + 2 * n, DP)

    def p_copy(j):
        return remote(stage.at[j], parts.at[d], p_send.at[j], p_recv.at[d], device_id=at(s, j))

    def join(j):
        rows = pl.ds(pl.multiple_of(j * TOK, TOK), TOK)
        part = jnp.dot(feat[rows, :], w[...], preferred_element_type=F32)

        @pl.when(j == d)
        def _():
            own_part[...] = part

        @pl.when(j != d)
        def _():
            stage[j] = part.astype(BF16)
            p_copy(j).start()

    def f_copy(j):
        rows = pl.ds(pl.multiple_of(j * TOK, TOK), TOK)
        return remote(feat.at[rows], feat.at[rows], f_send.at[j // 2], f_recv.at[j // 2], device_id=at(sib, d))

    def work(n, _):
        j = replica_of(home, n)
        slot = j // 2
        remote(
            stream.at[:, pl.ds(0, IN)], h0.at[slot], h_send.at[0], h_recv.at[slot], device_id=at(sib, d)
        ).wait_recv()

        @pl.when(j != d)
        def _():
            remote(packed, sc2.at[j], r2_send.at[0], r2_recv.at[j], device_id=at(s, j)).wait_recv()

        inv_j[...] = jnp.concatenate([sc2[j], jnp.zeros((128 - SECTIONS, 128), F32)], 0).T

        def one(t, _):
            r = pl.multiple_of((t // 2) * 32, 32)
            col = pl.multiple_of((t % 2) * 512, 512)
            cols = pl.ds(col, 512)
            taps = run_sections(
                h0[slot, pl.ds(r, 32), cols].astype(F32), inv_j[pl.ds(r, 32), :],
                lambda sec: gain_b[sec, :, cols], lambda sec: mix_b[sec, :, cols],
            )
            for i, tap in enumerate(taps):
                feat[pl.ds(pl.multiple_of(j * TOK + r, 32), 32), pl.ds(pl.multiple_of(i * IN + col, 512), 512)] = tap
            return 0

        lax.fori_loop(0, 8, one, 0)
        f_copy(j).start()
        join(j)
        return 0

    lax.fori_loop(1, 5, work, 0)

    def other(n, _):
        j = replica_of(jnp.logical_not(home), n)
        f_copy(j).wait_recv()
        join(j)
        return 0

    lax.fori_loop(1, 5, other, 0)

    up_copy.wait()

    def up_one(t, _):
        rows = pl.ds(pl.multiple_of(t * 32, 32), 32)
        taps = run_sections(
            up_in[rows, :].astype(F32), inv_own[rows, :], lambda sec: gain_u[sec], lambda sec: mix_u[sec]
        )
        upper[rows, :] = taps[2].astype(F32)
        return 0

    lax.fori_loop(0, 4, up_one, 0)

    def turn(t, _):
        rows = pl.ds(pl.multiple_of((t % 8) * TOK, TOK), TOK)
        cols = pl.ds(pl.multiple_of((t // 8) * 512, 512), 512)
        feat_t[cols, rows] = feat[rows, cols].T
        return 0

    lax.fori_loop(0, 48, turn, 0)

    for peer in dp_peers:
        remote(stage.at[peer], parts.at[peer], p_send.at[peer], p_recv.at[peer], device_id=at(s, peer)).wait_recv()

    inv_count = []
    for k in range(1, STEPS + 1):
        count = jnp.int32(0)
        for m in range(NMB):
            count = count + jnp.maximum(lengths[0, m] - k, 0)
        inv_count.append(1.0 / (jnp.full((1, 128), jnp.maximum(count, 1), jnp.int32).astype(F32) * D))

    def draft(q, _):
        cols = pl.ds(pl.multiple_of(q * 128, 128), 128)
        joined = own_part[:, cols]
        for peer in dp_peers:
            joined = joined + parts[peer, :, cols].astype(F32)
        up = upper[:, cols]
        dec = decay[:, cols]
        plen = left[...]

        def carry_of(k):
            return dec * mask_t[:, k - 1:k]

        state = joined
        pulls = []
        for k in range(1, STEPS + 1):
            state = joined + carry_of(k) * pltpu.roll(state, 1, 0)
            target = pltpu.roll(up, TOK - k, 0)
            diff = jnp.where(plen > k, state - target, 0.0)
            loss_acc[k - 1] += jnp.sum((diff * diff).reshape(TOK // 8, 8, 128), axis=0)
            pulls.append(diff * (2.0 * inv_count[k - 1]))
        back = pulls[STEPS - 1]
        total = back
        for k in range(STEPS - 1, 0, -1):
            back = pulls[k - 1] + pltpu.roll(carry_of(k + 1) * back, TOK - 1, 0)
            total = total + back
        total = total + pltpu.roll(carry_of(1) * back, TOK - 1, 0)
        rows_own[:, cols] = total.astype(BF16)
        return 0

    lax.fori_loop(0, OUT // 128, draft, 0)

    def q_copy(i):
        peer = lax.rem(d + i, DP)
        here = pl.ds(pl.multiple_of(d * TOK, TOK), TOK)
        return remote(rows_own, rows_all.at[here], q_send.at[i], q_recv.at[d], device_id=at(s, peer))

    for i in range(1, DP):
        q_copy(i).start()
    rows_all[pl.ds(pl.multiple_of(d * TOK, TOK), TOK), :] = rows_own[...]

    lane = lax.broadcasted_iota(jnp.int32, (8, 128), 1)
    losses = jnp.zeros((8, 128), F32)
    for k in range(1, STEPS + 1):
        losses = jnp.where(lane == k - 1, jnp.sum(loss_acc[k - 1]) * inv_count[k - 1], losses)
    loss_tile[...] = losses
    loss_all[s] = losses
    l_sends = []
    for i, peer in enumerate(seg_peers):
        copy = remote(loss_tile, loss_all.at[s], l_send.at[i], l_recv.at[s], device_id=at(peer, d))
        copy.start()
        l_sends.append(copy)

    for peer in dp_peers:
        there = pl.ds(pl.multiple_of(peer * TOK, TOK), TOK)
        remote(rows_own, rows_all.at[there], q_send.at[0], q_recv.at[peer], device_id=at(s, peer)).wait_recv()

    def o_copy(t):
        return pltpu.make_async_copy(
            grad.at[t], grad_out.at[t // 4, pl.ds(pl.multiple_of((t % 4) * 256, 256), 256)], o_sem.at[t]
        )

    def finish(t, _):
        rows = pl.ds(pl.multiple_of(t * 256, 256), 256)
        grad[t] = jnp.dot(feat_t[rows, :], rows_all[...], preferred_element_type=F32)
        o_copy(t).start()
        return 0

    lax.fori_loop(0, 12, finish, 0)

    for i, peer in enumerate(seg_peers):
        remote(loss_tile, loss_all.at[peer], l_send.at[i], l_recv.at[peer], device_id=at(peer, d)).wait_recv()
    summed = loss_all[0]
    for i in range(1, SEG):
        summed = summed + loss_all[i]
    loss_out[...] = summed

    for copy in g_sends + r1_sends + l_sends:
        copy.wait_send()

    @pl.when(home)
    def _():
        for i in range(1, DP):
            h_copy(i).wait_send()
            r2_copy(i).wait_send()

    for n in range(1, 5):
        f_copy(replica_of(home, n)).wait_send()
    for peer in dp_peers:
        p_copy(peer).wait_send()
    for i in range(1, DP):
        q_copy(i).wait_send()
    for t in range(12):
        o_copy(t).wait()


def local(stream_in, sec_gain, sec_mix, fc_weight, decay, lengths, ttt_mask):
    vmem = pltpu.VMEM
    dma = pltpu.SemaphoreType.DMA
    scratch = [
        vmem((SECTIONS, 1, D), F32), vmem((SECTIONS, 1, D), F32),
        vmem((SECTIONS, 8, IN), F32), vmem((SECTIONS, 8, IN), F32),
        vmem((SECTIONS, 8, OUT), F32), vmem((SECTIONS, 8, OUT), F32),
        vmem((16, D), BF16), vmem((16, D), F32),
        vmem((4, TOK, IN), BF16),
        vmem((OWN, 128), F32), vmem((SEG, OWN, 128), F32),
        vmem((SECTIONS, 128), F32), vmem((DP, SECTIONS, 128), F32),
        vmem((TOK, 128), F32), vmem((TOK, 128), F32),
        vmem((3 * IN, OUT), BF16),
        vmem((DP * TOK, 3 * IN), BF16), vmem((3 * IN, DP * TOK), BF16),
        vmem((DP, TOK, OUT), BF16), vmem((DP, TOK, OUT), BF16), vmem((TOK, OUT), F32),
        vmem((TOK, OUT), BF16), vmem((TOK, OUT), F32),
        vmem((TOK, 128), F32), vmem((TOK, 128), F32), vmem((TOK, 128), jnp.int32),
        vmem((STEPS, 8, 128), F32), vmem((8, 128), F32), vmem((SEG, 8, 128), F32),
        vmem((TOK, OUT), BF16), vmem((DP * TOK, OUT), BF16),
        vmem((12, 256, OUT), F32),
        dma((5,)), dma((8,)), dma((8,)), dma((SEG,)), dma((SEG,)), dma((8,)), dma((8,)),
        dma((DP,)), dma((4,)), dma((SEG,)), dma((SEG,)), dma((DP,)), dma((DP,)), dma((4,)), dma((4,)),
        dma((DP,)), dma((DP,)), dma((DP,)), dma((DP,)), dma((SEG,)), dma((SEG,)), dma((12,)),
    ]
    any_space = pl.BlockSpec(memory_space=pl.ANY)
    in_vmem = pl.BlockSpec(memory_space=pltpu.VMEM)
    loss, grad = pl.pallas_call(
        kernel,
        out_shape=(
            jax.ShapeDtypeStruct((8, 128), F32),
            jax.ShapeDtypeStruct((3, IN, OUT), F32),
        ),
        in_specs=[any_space, any_space, any_space, any_space, in_vmem,
                  pl.BlockSpec(memory_space=pltpu.SMEM), in_vmem],
        out_specs=(in_vmem, any_space),
        scratch_shapes=scratch,
        compiler_params=pltpu.CompilerParams(
            collective_id=0, has_side_effects=True, vmem_limit_bytes=56 * 1024 * 1024
        ),
        name="window",
    )(stream_in, sec_gain, sec_mix, fc_weight, decay.reshape(1, OUT), lengths, ttt_mask)
    return loss[0:1, 0:STEPS], grad


def solution(mesh):
    in_specs = (
        P("dp", None),
        P("segment", None),
        P("segment", None),
        P(None, "dp", "segment"),
        P("segment"),
        P("dp", None),
        P(None, "dp"),
    )
    out_specs = (P("dp", None), P(None, "dp", "segment"))
    return jax.shard_map(local, mesh=mesh, in_specs=in_specs, out_specs=out_specs, check_vma=False)
```

```python
import functools

import jax
import jax.numpy as jnp
from jax import lax
from jax.experimental import pallas as pl
from jax.experimental.pallas import tpu as pltpu
from jax.sharding import PartitionSpec as P

D = 8192
MB = 16
NMB = 8
STEPS = 7
SECTIONS = 16
TAPS = (0, SECTIONS // 2, SECTIONS - 1)
TOK = 128
SEG = 16
DP = 8
VM1 = 40
VM2 = 32
IN = D // DP
OUT = D // SEG
OWN = TOK // SEG
HALF = OUT // 2
F32 = jnp.float32
BF16 = jnp.bfloat16
MESH = pl.DeviceIdType.MESH


def at(segment, dp):
    return {"segment": segment, "dp": dp}


def advance(h, half_gain, mix, inv):
    u = (h * half_gain) * inv
    return (h + (mix * u) * (1.0 + jnp.tanh(u))).astype(BF16)


def run_sections(h, inv_cols, gain_of, mix_of):
    rows = h.shape[0]
    taps = []
    for sec in range(SECTIONS):
        gain = jnp.concatenate([gain_of(sec)] * (rows // 8), 0)
        mix = jnp.concatenate([mix_of(sec)] * (rows // 8), 0)
        out = advance(h, gain, mix, inv_cols[:, sec:sec + 1])
        if sec in TAPS:
            taps.append(out)
        h = out.astype(F32)
    return taps


def kernel(stream, gain, mix, weight, decay_in, lengths_in, mask_in, loss_out, feat_t, rows_out,
           decay, lengths, mask, params, gain_b, mix_b, gain_u, mix_u, rows16, hx, h0, tile, sc1, packed, sc2, inv_own, inv_j,
           w, feat, stage, keep_a, keep_b, in_a1, in_b1, out_a2, in_a2, out_b2, in_b2, own,
           up_in, upper, mask_t, mask_pad, left, loss_acc, loss_tile, loss_all, rows_all,
           in_sem, g_send, g_recv, gf_send, h_send, h_recv, r1_send, r1_recv, r2_send, r2_recv, f_send, f_recv,
           a1_send, a1_recv, b1_send, b1_recv, a2_send, a2_recv, b2_send, b2_recv,
           q_send, q_recv, qa_send, qa_recv, qb_send, qb_recv, l_send, l_recv):
    s = lax.axis_index("segment")
    d = lax.axis_index("dp")
    c = lax.rem(s, 2)
    y = d // 2
    zh = lax.rem(d, 2)
    pair = d + 1 - 2 * zh
    sib = s + 1 - 2 * c
    home = zh == c
    seg_peers = [lax.rem(s + i, SEG) for i in range(1, SEG)]
    dp_peers = [lax.rem(d + i, DP) for i in range(1, DP)]
    y_peers = [lax.rem(y + i, 4) for i in range(1, 4)]
    plane = (s // 8) * 8
    x_peers = [plane + lax.rem(s - plane + 2 * i, 8) for i in range(1, 4)]
    across = lax.rem(s + 8, SEG)
    remote = functools.partial(pltpu.make_async_remote_copy, device_id_type=MESH)

    gain_copy = pltpu.make_async_copy(gain, params.at[s, 0], in_sem.at[5])
    mix_copy = pltpu.make_async_copy(mix, params.at[s, 1], in_sem.at[6])
    gain_copy.start()
    mix_copy.start()
    w_copies = [
        pltpu.make_async_copy(weight.at[i], w.at[pl.ds(i * IN, IN)], in_sem.at[i]) for i in range(3)
    ]
    row0 = pl.multiple_of((s // 2) * 16, 16)
    rows_copy = pltpu.make_async_copy(stream.at[pl.ds(row0, 16)], rows16, in_sem.at[3])
    up_copy = pltpu.make_async_copy(
        stream.at[:, pl.ds(pl.multiple_of(s * OUT, OUT), OUT)], up_in, in_sem.at[4]
    )
    small = [
        pltpu.make_async_copy(src, dst, in_sem.at[7 + i])
        for i, (src, dst) in enumerate(((decay_in, decay), (lengths_in, lengths), (mask_in, mask)))
    ]
    rows_copy.start()
    for copy in small:
        copy.start()

    barrier = pltpu.get_barrier_semaphore()
    for peer in seg_peers:
        pl.semaphore_signal(barrier, inc=1, device_id=at(peer, d), device_id_type=MESH)
    for peer in dp_peers:
        pl.semaphore_signal(barrier, inc=1, device_id=at(s, peer), device_id_type=MESH)
    gain_copy.wait()
    mix_copy.wait()
    pl.semaphore_wait(barrier, SEG - 1 + DP - 1)

    def g_copy(slot, peer, send):
        return remote(params.at[slot], params.at[slot], send, g_recv.at[slot], device_id=at(peer, d))

    sends = []

    def post(copy):
        copy.start()
        sends.append(copy)

    for i, peer in enumerate([across] + x_peers + [sib]):
        post(g_copy(s, peer, g_send.at[i]))

    def h_copy(i):
        peer = lax.rem(d + i, DP)
        return remote(
            stream.at[:, pl.ds(pl.multiple_of(peer * IN, IN), IN)], h0.at[d // 2],
            h_send.at[i], h_recv.at[d // 2], device_id=at(s, peer),
        )

    @pl.when(home)
    def _():
        for i in range(1, DP):
            h_copy(i).start()
        pltpu.make_async_copy(
            stream.at[:, pl.ds(pl.multiple_of(d * IN, IN), IN)], h0.at[d // 2], h_recv.at[d // 2]
        ).start()

    up_copy.start()
    for copy in w_copies:
        copy.start()

    def wait_param(slot):
        g_copy(slot, sib, g_send.at[0]).wait_recv()

    wait_param(across)
    for i, peer in enumerate(x_peers + [sib]):
        post(g_copy(across, peer, gf_send.at[i]))

    for copy in small:
        copy.wait()
    token = lax.broadcasted_iota(jnp.int32, (TOK, 128), 0)
    pos = token & (MB - 1)
    micro = lax.shift_right_logical(token, 4)
    tok_len = jnp.zeros((TOK, 128), jnp.int32)
    for m in range(NMB):
        tok_len = jnp.where(micro == m, lengths[0, m], tok_len)
    left[...] = tok_len - pos
    mask_pad[...] = jnp.zeros_like(mask_pad)
    mask_pad[0:STEPS, :] = mask[...].astype(F32)
    mask_t[...] = jnp.where(pos >= 1, mask_pad[...].T, 0.0)
    loss_acc[...] = jnp.zeros_like(loss_acc)
    rows_copy.wait()
    hx[...] = rows16[...].astype(F32)

    for i, slot in enumerate(x_peers):
        wait_param(slot)
        post(g_copy(slot, sib, gf_send.at[4 + i]))
    for i, peer in enumerate(x_peers):
        slot = lax.rem(peer + 8, SEG)
        wait_param(slot)
        post(g_copy(slot, sib, gf_send.at[7 + i]))
    for i in range(SEG // 2):
        wait_param(lax.rem(sib + 2 * i, SEG))

    half = pl.ds(pl.multiple_of(c * OWN, OWN), OWN)
    lane = lax.broadcasted_iota(jnp.int32, (OWN, 128), 1)

    def inverse(h):
        return lax.rsqrt(jnp.sum(h * h, axis=1, keepdims=True) * (1.0 / D) + 1e-05)

    def scale_step(sec, carry):
        inv, acc = carry
        acc = jnp.where(lane == sec, inv, acc)
        h = advance(hx[half, :], 0.5 * params[sec, 0], params[sec, 1], inv).astype(F32)
        hx[half, :] = h
        return inverse(h), acc

    inv, acc = lax.fori_loop(
        0, SECTIONS - 1, scale_step, (inverse(hx[half, :]), jnp.zeros((OWN, 128), F32))
    )
    tile[...] = jnp.where(lane == SECTIONS - 1, inv, acc)
    sc1[s] = tile[...]
    for i, peer in enumerate(seg_peers):
        post(remote(tile, sc1.at[s], r1_send.at[i], r1_recv.at[s], device_id=at(peer, d)))

    def spread(sec, _):
        mine = pl.ds(pl.multiple_of(d * IN, IN), IN)
        loss_cols = pl.ds(pl.multiple_of(s * OUT, OUT), OUT)
        gain_b[sec] = jnp.broadcast_to(0.5 * params[sec, 0, :, mine], (8, IN))
        mix_b[sec] = jnp.broadcast_to(params[sec, 1, :, mine], (8, IN))
        gain_u[sec] = jnp.broadcast_to(0.5 * params[sec, 0, :, loss_cols], (8, OUT))
        mix_u[sec] = jnp.broadcast_to(params[sec, 1, :, loss_cols], (8, OUT))
        return 0

    lax.fori_loop(0, SECTIONS, spread, 0)
    for i, peer in enumerate(seg_peers):
        remote(tile, sc1.at[peer], r1_send.at[i], r1_recv.at[peer], device_id=at(peer, d)).wait_recv()
    inv_own[...] = sc1[...].reshape(TOK, 128)
    packed[...] = inv_own[...].T[0:SECTIONS, :]

    def r2_copy(i):
        peer = lax.rem(d + i, DP)
        return remote(packed, sc2.at[d], r2_send.at[i], r2_recv.at[d], device_id=at(s, peer))

    @pl.when(home)
    def _():
        for i in range(1, DP):
            r2_copy(i).start()
        sc2[d] = packed[...]

    for copy in w_copies:
        copy.wait()

    first, second = pl.ds(0, HALF), pl.ds(HALF, HALF)

    def replica_of(parity, n):
        return lax.rem(y + n, 4) * 2 + parity

    def a1_copy(to_y):
        j = to_y * 2 + 1 - zh
        return remote(
            stage.at[j, :, first], in_a1.at[to_y], a1_send.at[to_y], a1_recv.at[to_y], device_id=at(s, pair)
        )

    def b1_copy(to_y, z):
        j = to_y * 2 + z
        return remote(
            stage.at[j, :, second], in_b1.at[y * 2 + z], b1_send.at[j], b1_recv.at[y * 2 + z],
            device_id=at(s, to_y * 2 + zh),
        )

    def a2_copy(to_y):
        return remote(
            out_a2.at[to_y], in_a2.at[y], a2_send.at[to_y], a2_recv.at[y], device_id=at(s, to_y * 2 + zh)
        )

    def b2_copy():
        return remote(out_b2, in_b2, b2_send.at[0], b2_recv.at[0], device_id=at(s, pair))

    def join(j, z):
        to_y = j // 2
        rows = pl.ds(pl.multiple_of(j * TOK, TOK), TOK)
        part = jnp.dot(feat[rows, :], w[...], preferred_element_type=F32)
        stage[j] = part.astype(BF16)

        @pl.when(z == zh)
        def _():
            keep_a[to_y] = part[:, 0:HALF]

        @pl.when(z != zh)
        def _():
            a1_copy(to_y).start()

        @pl.when(to_y == y)
        def _():
            keep_b[z] = part[:, HALF:OUT]

        @pl.when(to_y != y)
        def _():
            b1_copy(to_y, z).start()

    def f_copy(j):
        rows = pl.ds(pl.multiple_of(j * TOK, TOK), TOK)
        return remote(feat.at[rows], feat.at[rows], f_send.at[j // 2], f_recv.at[j // 2], device_id=at(sib, d))

    def work(n, _):
        j = replica_of(c, n)
        slot = j // 2
        remote(
            stream.at[:, pl.ds(0, IN)], h0.at[slot], h_send.at[0], h_recv.at[slot], device_id=at(sib, d)
        ).wait_recv()

        @pl.when(j != d)
        def _():
            remote(packed, sc2.at[j], r2_send.at[0], r2_recv.at[j], device_id=at(s, j)).wait_recv()

        inv_j[...] = jnp.concatenate([sc2[j], jnp.zeros((128 - SECTIONS, 128), F32)], 0).T

        def one(t, _):
            r = pl.multiple_of((t // 2) * 32, 32)
            col = pl.multiple_of((t % 2) * 512, 512)
            cols = pl.ds(col, 512)
            taps = run_sections(
                h0[slot, pl.ds(r, 32), cols].astype(F32), inv_j[pl.ds(r, 32), :],
                lambda sec: gain_b[sec, :, cols], lambda sec: mix_b[sec, :, cols],
            )
            for i, tap in enumerate(taps):
                feat[pl.ds(pl.multiple_of(j * TOK + r, 32), 32), pl.ds(pl.multiple_of(i * IN + col, 512), 512)] = tap
            return 0

        lax.fori_loop(0, 8, one, 0)
        f_copy(j).start()
        join(j, c)
        return 0

    lax.fori_loop(1, 5, work, 0)

    def other(n, _):
        j = replica_of(1 - c, n)
        f_copy(j).wait_recv()
        join(j, 1 - c)
        return 0

    lax.fori_loop(1, 5, other, 0)

    up_copy.wait()

    def up_one(t, _):
        rows = pl.ds(pl.multiple_of(t * 32, 32), 32)
        taps = run_sections(
            up_in[rows, :].astype(F32), inv_own[rows, :], lambda sec: gain_u[sec], lambda sec: mix_u[sec]
        )
        upper[rows, :] = taps[2].astype(F32)
        return 0

    lax.fori_loop(0, 4, up_one, 0)

    for i in range(1, 5):
        to_y = lax.rem(y + i, 4)
        remote(
            stage.at[0, :, first], in_a1.at[to_y], a1_send.at[to_y], a1_recv.at[to_y], device_id=at(s, pair)
        ).wait_recv()
        total = keep_a[to_y] + in_a1[to_y].astype(F32)
        if i < 4:
            out_a2[to_y] = total.astype(BF16)
            post(a2_copy(to_y))
        else:
            own[:, 0:HALF] = total

    for step in range(2):
        z = 1 - zh if step == 0 else zh
        total = keep_b[z]
        for from_y in y_peers:
            slot = from_y * 2 + z
            remote(
                stage.at[0, :, second], in_b1.at[slot], b1_send.at[slot], b1_recv.at[slot],
                device_id=at(s, from_y * 2 + zh),
            ).wait_recv()
            total = total + in_b1[slot].astype(F32)
        if step == 0:
            out_b2[...] = total.astype(BF16)
            post(b2_copy())
        else:
            own[:, HALF:OUT] = total

    def turn(t, _):
        rows = pl.ds(pl.multiple_of((t % 8) * TOK, TOK), TOK)
        cols = pl.ds(pl.multiple_of((t // 8) * 512, 512), 512)
        feat_t[cols, rows] = feat[rows, cols].T
        return 0

    lax.fori_loop(0, 48, turn, 0)

    inv_count = []
    for k in range(1, STEPS + 1):
        count = jnp.int32(0)
        for m in range(NMB):
            count = count + jnp.maximum(lengths[0, m] - k, 0)
        inv_count.append(1.0 / (jnp.full((1, 128), jnp.maximum(count, 1), jnp.int32).astype(F32) * D))

    here = pl.ds(pl.multiple_of(d * TOK, TOK), TOK)

    def draft(q, _):
        cols = pl.ds(pl.multiple_of(q * 128, 128), 128)
        joined = own[:, cols]
        up = upper[:, cols]
        dec = decay[:, cols]
        plen = left[...]

        def carry_of(k):
            return dec * mask_t[:, k - 1:k]

        state = joined
        pulls = []
        for k in range(1, STEPS + 1):
            state = joined + carry_of(k) * pltpu.roll(state, 1, 0)
            target = pltpu.roll(up, TOK - k, 0)
            diff = jnp.where(plen > k, state - target, 0.0)
            loss_acc[k - 1] += jnp.sum((diff * diff).reshape(TOK // 8, 8, 128), axis=0)
            pulls.append(diff * (2.0 * inv_count[k - 1]))
        back = pulls[STEPS - 1]
        total = back
        for k in range(STEPS - 1, 0, -1):
            back = pulls[k - 1] + pltpu.roll(carry_of(k + 1) * back, TOK - 1, 0)
            total = total + back
        total = total + pltpu.roll(carry_of(1) * back, TOK - 1, 0)
        rows_all[here, cols] = total.astype(BF16)
        return 0

    def rows_of(j):
        return pl.ds(pl.multiple_of(j * TOK, TOK), TOK)

    def q_copy(part, i, source, peer):
        block = rows_all.at[rows_of(source), first if part == 0 else second]
        return remote(block, block, q_send.at[part * 4 + i], q_recv.at[part * DP + source], device_id=at(s, peer))

    def qa_copy(i, from_y, to_y):
        block = rows_all.at[rows_of(from_y * 2 + 1 - zh), first]
        return remote(block, block, qa_send.at[i], qa_recv.at[from_y], device_id=at(s, to_y * 2 + zh))

    def qb_copy(i, from_y, z):
        block = rows_all.at[rows_of(from_y * 2 + z), second]
        return remote(block, block, qb_send.at[i], qb_recv.at[from_y], device_id=at(s, pair))

    for i, from_y in enumerate(y_peers):
        remote(
            out_a2.at[0], in_a2.at[from_y], a2_send.at[0], a2_recv.at[from_y], device_id=at(s, from_y * 2 + zh)
        ).wait_recv()
        own[:, 0:HALF] += in_a2[from_y].astype(F32)
    lax.fori_loop(0, 2, draft, 0)
    for i, peer in enumerate([pair] + [p * 2 + zh for p in y_peers]):
        post(q_copy(0, i, d, peer))
    b2_copy().wait_recv()
    own[:, HALF:OUT] += in_b2[...].astype(F32)
    lax.fori_loop(2, 4, draft, 0)
    for i, peer in enumerate([pair] + [p * 2 + zh for p in y_peers]):
        post(q_copy(1, i, d, peer))

    q_copy(0, 0, pair, pair).wait_recv()
    for i, to_y in enumerate(y_peers):
        post(qa_copy(i, y, to_y))

    lane = lax.broadcasted_iota(jnp.int32, (8, 128), 1)
    losses = jnp.zeros((8, 128), F32)
    for k in range(1, STEPS + 1):
        losses = jnp.where(lane == k - 1, jnp.sum(loss_acc[k - 1]) * inv_count[k - 1], losses)
    loss_tile[...] = losses
    loss_all[s] = losses
    for i, peer in enumerate(seg_peers):
        post(remote(loss_tile, loss_all.at[s], l_send.at[i], l_recv.at[s], device_id=at(peer, d)))

    for i, from_y in enumerate(y_peers):
        q_copy(1, 0, from_y * 2 + zh, pair).wait_recv()
        post(qb_copy(i, from_y, zh))

    for i, peer in enumerate(seg_peers):
        remote(loss_tile, loss_all.at[peer], l_send.at[i], l_recv.at[peer], device_id=at(peer, d)).wait_recv()
    summed = loss_all[0]
    for i in range(1, SEG):
        summed = summed + loss_all[i]
    loss_out[...] = summed

    q_copy(1, 0, pair, pair).wait_recv()
    for from_y in y_peers:
        q_copy(0, 0, from_y * 2 + zh, pair).wait_recv()
        qa_copy(0, from_y, from_y).wait_recv()
        qb_copy(0, from_y, 1 - zh).wait_recv()
    rows_copy = pltpu.make_async_copy(rows_all, rows_out, in_sem.at[0])
    rows_copy.start()

    for copy in sends:
        copy.wait_send()

    @pl.when(home)
    def _():
        for i in range(1, DP):
            h_copy(i).wait_send()
            r2_copy(i).wait_send()

    for n in range(1, 5):
        f_copy(replica_of(c, n)).wait_send()
    for to_y in range(4):
        a1_copy(to_y).wait_send()
    for to_y in y_peers:
        for z in range(2):
            b1_copy(to_y, z).wait_send()
    rows_copy.wait()


def gradient(feat_t, rows, loss, grad_out, loss_out, grad, sem):
    def out_copy(t):
        return pltpu.make_async_copy(
            grad.at[t], grad_out.at[pl.ds(pl.multiple_of(t * 256, 256), 256)], sem.at[t]
        )

    def one(t, _):
        block = pl.ds(pl.multiple_of(t * 256, 256), 256)
        grad[t] = jnp.dot(feat_t[block, :], rows[...], preferred_element_type=F32)
        out_copy(t).start()
        return 0

    lax.fori_loop(0, 12, one, 0)
    loss_out[...] = loss[0:1, 0:STEPS]
    for t in range(12):
        out_copy(t).wait()


def local(stream_in, sec_gain, sec_mix, fc_weight, decay, lengths, ttt_mask):
    vmem = pltpu.VMEM
    dma = pltpu.SemaphoreType.DMA
    scratch = [
        vmem((1, OUT), F32), pltpu.SMEM((1, NMB), jnp.int32), vmem((STEPS, TOK), jnp.int32),
        vmem((SECTIONS, 2, 1, D), F32),
        vmem((SECTIONS, 8, IN), F32), vmem((SECTIONS, 8, IN), F32),
        vmem((SECTIONS, 8, OUT), F32), vmem((SECTIONS, 8, OUT), F32),
        vmem((16, D), BF16), vmem((16, D), F32),
        vmem((4, TOK, IN), BF16),
        vmem((OWN, 128), F32), vmem((SEG, OWN, 128), F32),
        vmem((SECTIONS, 128), F32), vmem((DP, SECTIONS, 128), F32),
        vmem((TOK, 128), F32), vmem((TOK, 128), F32),
        vmem((3 * IN, OUT), BF16),
        vmem((DP * TOK, 3 * IN), BF16),
        vmem((DP, TOK, OUT), BF16), vmem((4, TOK, HALF), F32), vmem((2, TOK, HALF), F32),
        vmem((4, TOK, HALF), BF16), vmem((DP, TOK, HALF), BF16),
        vmem((4, TOK, HALF), BF16), vmem((4, TOK, HALF), BF16),
        vmem((TOK, HALF), BF16), vmem((TOK, HALF), BF16), vmem((TOK, OUT), F32),
        vmem((TOK, OUT), BF16), vmem((TOK, OUT), F32),
        vmem((TOK, 128), F32), vmem((TOK, 128), F32), vmem((TOK, 128), jnp.int32),
        vmem((STEPS, 8, 128), F32), vmem((8, 128), F32), vmem((SEG, 8, 128), F32),
        vmem((DP * TOK, OUT), BF16),
        dma((10,)), dma((5,)), dma((SEG,)), dma((10,)), dma((DP,)), dma((4,)),
        dma((SEG,)), dma((SEG,)), dma((DP,)), dma((DP,)), dma((4,)), dma((4,)),
        dma((4,)), dma((4,)), dma((DP,)), dma((DP,)), dma((4,)), dma((4,)), dma((1,)), dma((1,)),
        dma((8,)), dma((2 * DP,)), dma((3,)), dma((4,)), dma((3,)), dma((4,)), dma((SEG,)), dma((SEG,)),
    ]
    any_space = pl.BlockSpec(memory_space=pl.ANY)
    in_hbm = pl.BlockSpec(memory_space=pltpu.HBM)
    in_vmem = pl.BlockSpec(memory_space=pltpu.VMEM)
    loss, feat_t, rows = pl.pallas_call(
        kernel,
        out_shape=(
            jax.ShapeDtypeStruct((8, 128), F32),
            jax.ShapeDtypeStruct((3 * IN, DP * TOK), BF16),
            jax.ShapeDtypeStruct((DP * TOK, OUT), BF16),
        ),
        in_specs=[in_hbm] * 7,
        out_specs=(in_vmem, in_vmem, any_space),
        scratch_shapes=scratch,
        compiler_params=pltpu.CompilerParams(
            collective_id=0, has_side_effects=True, vmem_limit_bytes=VM1 * 1024 * 1024
        ),
        name="window",
    )(stream_in, sec_gain, sec_mix, fc_weight, decay.reshape(1, OUT), lengths, ttt_mask)
    grad, step_loss = pl.pallas_call(
        gradient,
        out_shape=(
            jax.ShapeDtypeStruct((3 * IN, OUT), F32),
            jax.ShapeDtypeStruct((1, STEPS), F32),
        ),
        in_specs=[in_vmem] * 3,
        out_specs=(any_space, in_vmem),
        scratch_shapes=[vmem((12, 256, OUT), F32), dma((12,))],
        compiler_params=pltpu.CompilerParams(vmem_limit_bytes=VM2 * 1024 * 1024),
        name="gradient",
    )(feat_t, rows, loss)
    return step_loss, grad.reshape(3, IN, OUT)


def solution(mesh):
    in_specs = (
        P("dp", None),
        P("segment", None),
        P("segment", None),
        P(None, "dp", "segment"),
        P("segment"),
        P("dp", None),
        P(None, "dp"),
    )
    out_specs = (P("dp", None), P(None, "dp", "segment"))
    return jax.shard_map(local, mesh=mesh, in_specs=in_specs, out_specs=out_specs, check_vma=False)
```

```python
import functools

import jax
import jax.numpy as jnp
from jax import lax
from jax.experimental import pallas as pl
from jax.experimental.pallas import tpu as pltpu
from jax.sharding import PartitionSpec as P

D = 8192
MB = 16
NMB = 8
STEPS = 7
SECTIONS = 16
TAPS = (0, SECTIONS // 2, SECTIONS - 1)
TOK = 128
SEG = 16
DP = 8
VM1 = 56
VM2 = 56
IN = D // DP
OUT = D // SEG
OWN = TOK // SEG
HALF = OUT // 2
F32 = jnp.float32
BF16 = jnp.bfloat16
MESH = pl.DeviceIdType.MESH


def at(segment, dp):
    return {"segment": segment, "dp": dp}


def advance(h, half_gain, mix, inv):
    u = (h * half_gain) * inv
    return (h + (mix * u) * (1.0 + jnp.tanh(u))).astype(BF16)


def run_sections(h, inv_of, gain_of, mix_of):
    rows, cols = h.shape
    taps = []
    for sec in range(SECTIONS):
        gain = jnp.concatenate([gain_of(sec)] * (rows // 8), 0)
        mix = jnp.concatenate([mix_of(sec)] * (rows // 8), 0)
        out = advance(h, gain, mix, jnp.concatenate([inv_of(sec)] * (cols // 128), 1))
        if sec in TAPS:
            taps.append(out)
        h = out.astype(F32)
    return taps


def kernel(stream, gain, mix, weight, decay_in, lengths_in, mask_in, loss_out, feat_out, rows_out,
           decay, lengths, mask, params, gain_b, mix_b, gain_u, mix_u, rows16, hx, h0, tile, sc1, packed, sc2, inv_own, inv_b,
           w, feat, feat_t, stage, keep_a, keep_b, in_a1, in_b1, out_a2, in_a2, out_b2, in_b2, own,
           up_in, upper, mask_t, mask_pad, left, loss_acc, loss_tile, loss_all, rows_all,
           in_sem, g_send, g_recv, gf_send, h_send, h_recv, r1_send, r1_recv, r2_send, r2_recv, f_send, f_recv,
           a1_send, a1_recv, b1_send, b1_recv, a2_send, a2_recv, b2_send, b2_recv,
           q_send, q_recv, qa_send, qa_recv, qb_send, qb_recv, l_send, l_recv, o_sem):
    s = lax.axis_index("segment")
    d = lax.axis_index("dp")
    c = lax.rem(s, 2)
    y = d // 2
    zh = lax.rem(d, 2)
    pair = d + 1 - 2 * zh
    sib = s + 1 - 2 * c
    home = zh == c
    seg_peers = [lax.rem(s + i, SEG) for i in range(1, SEG)]
    y_peers = [lax.rem(y + i, 4) for i in range(1, 4)]
    plane = (s // 8) * 8
    x_peers = [plane + lax.rem(s - plane + 2 * i, 8) for i in range(1, 4)]
    across = lax.rem(s + 8, SEG)
    far = [(s, p * 2 + zh) for p in y_peers]
    far = [(across, lax.rem(y + i, 4) * 2 + 1 - zh) for i in (2, 1, 3, 0)] + far
    remote = functools.partial(pltpu.make_async_remote_copy, device_id_type=MESH)

    gain_copy = pltpu.make_async_copy(gain, params.at[s, 0], in_sem.at[5])
    mix_copy = pltpu.make_async_copy(mix, params.at[s, 1], in_sem.at[6])
    gain_copy.start()
    mix_copy.start()
    w_copies = [
        pltpu.make_async_copy(weight.at[i], w.at[pl.ds(i * IN, IN)], in_sem.at[i]) for i in range(3)
    ]
    row0 = pl.multiple_of((s // 2) * 16, 16)
    rows_copy = pltpu.make_async_copy(stream.at[pl.ds(row0, 16)], rows16, in_sem.at[3])
    up_copy = pltpu.make_async_copy(
        stream.at[:, pl.ds(pl.multiple_of(s * OUT, OUT), OUT)], up_in, in_sem.at[4]
    )
    small = [
        pltpu.make_async_copy(src, dst, in_sem.at[7 + i])
        for i, (src, dst) in enumerate(((decay_in, decay), (lengths_in, lengths), (mask_in, mask)))
    ]
    rows_copy.start()
    for copy in small:
        copy.start()

    barrier = pltpu.get_barrier_semaphore()
    for peer in seg_peers:
        pl.semaphore_signal(barrier, inc=1, device_id=at(peer, d), device_id_type=MESH)
    for seg, peer in far + [(s, pair)]:
        pl.semaphore_signal(barrier, inc=1, device_id=at(seg, peer), device_id_type=MESH)
    gain_copy.wait()
    mix_copy.wait()
    pl.semaphore_wait(barrier, SEG - 1 + DP)

    def g_copy(slot, peer, send):
        return remote(params.at[slot], params.at[slot], send, g_recv.at[slot], device_id=at(peer, d))

    sends = []

    def post(copy):
        copy.start()
        sends.append(copy)

    for i, peer in enumerate([across] + x_peers + [sib]):
        post(g_copy(s, peer, g_send.at[i]))

    def h_copy(i):
        seg, peer = far[i]
        return remote(
            stream.at[:, pl.ds(pl.multiple_of(peer * IN, IN), IN)], h0.at[y],
            h_send.at[i], h_recv.at[y], device_id=at(seg, peer),
        )

    @pl.when(home)
    def _():
        for i in range(DP - 1):
            h_copy(i).start()
        pltpu.make_async_copy(
            stream.at[:, pl.ds(pl.multiple_of(d * IN, IN), IN)], h0.at[y], h_recv.at[y]
        ).start()

    up_copy.start()
    for copy in w_copies:
        copy.start()

    def wait_param(slot):
        g_copy(slot, sib, g_send.at[0]).wait_recv()

    wait_param(across)
    for i, peer in enumerate(x_peers + [sib]):
        post(g_copy(across, peer, gf_send.at[i]))

    for copy in small:
        copy.wait()
    token = lax.broadcasted_iota(jnp.int32, (TOK, 128), 0)
    pos = token & (MB - 1)
    micro = lax.shift_right_logical(token, 4)
    tok_len = jnp.zeros((TOK, 128), jnp.int32)
    for m in range(NMB):
        tok_len = jnp.where(micro == m, lengths[0, m], tok_len)
    left[...] = tok_len - pos
    mask_pad[...] = jnp.zeros_like(mask_pad)
    mask_pad[0:STEPS, :] = mask[...].astype(F32)
    mask_t[...] = jnp.where(pos >= 1, mask_pad[...].T, 0.0)
    loss_acc[...] = jnp.zeros_like(loss_acc)
    rows_copy.wait()
    hx[...] = rows16[...].astype(F32)

    for i, slot in enumerate(x_peers):
        wait_param(slot)
        post(g_copy(slot, sib, gf_send.at[4 + i]))
    for i, peer in enumerate(x_peers):
        slot = lax.rem(peer + 8, SEG)
        wait_param(slot)
        post(g_copy(slot, sib, gf_send.at[7 + i]))
    for i in range(SEG // 2):
        wait_param(lax.rem(sib + 2 * i, SEG))

    half = pl.ds(pl.multiple_of(c * OWN, OWN), OWN)
    lane = lax.broadcasted_iota(jnp.int32, (OWN, 128), 1)

    def inverse(h):
        return lax.rsqrt(jnp.sum(h * h, axis=1, keepdims=True) * (1.0 / D) + 1e-05)

    def scale_step(sec, carry):
        inv, acc = carry
        acc = jnp.where(lane == sec, inv, acc)
        h = advance(hx[half, :], 0.5 * params[sec, 0], params[sec, 1], inv).astype(F32)
        hx[half, :] = h
        return inverse(h), acc

    inv, acc = lax.fori_loop(
        0, SECTIONS - 1, scale_step, (inverse(hx[half, :]), jnp.zeros((OWN, 128), F32))
    )
    tile[...] = jnp.where(lane == SECTIONS - 1, inv, acc)
    sc1[s] = tile[...]
    chips = [lax.rem(s // 2 + i, SEG // 2) * 2 for i in range(1, SEG // 2)]
    for i, peer in enumerate([p + zh for p in chips] + [sib] + [p + 1 - zh for p in chips]):
        post(remote(tile, sc1.at[s], r1_send.at[i], r1_recv.at[s], device_id=at(peer, d)))

    def spread(sec, _):
        mine = pl.ds(pl.multiple_of(d * IN, IN), IN)
        loss_cols = pl.ds(pl.multiple_of(s * OUT, OUT), OUT)
        gain_b[sec] = jnp.broadcast_to(0.5 * params[sec, 0, :, mine], (8, IN))
        mix_b[sec] = jnp.broadcast_to(params[sec, 1, :, mine], (8, IN))
        gain_u[sec] = jnp.broadcast_to(0.5 * params[sec, 0, :, loss_cols], (8, OUT))
        mix_u[sec] = jnp.broadcast_to(params[sec, 1, :, loss_cols], (8, OUT))
        return 0

    lax.fori_loop(0, SECTIONS, spread, 0)
    for i, peer in enumerate(seg_peers):
        remote(tile, sc1.at[peer], r1_send.at[i], r1_recv.at[peer], device_id=at(peer, d)).wait_recv()
    inv_own[...] = sc1[...].reshape(TOK, 128)
    packed[...] = inv_own[...].T[0:SECTIONS, :]

    def r2_copy(i):
        seg, peer = far[i]
        return remote(packed, sc2.at[d], r2_send.at[i], r2_recv.at[d], device_id=at(seg, peer))

    @pl.when(home)
    def _():
        for i in range(DP - 1):
            r2_copy(i).start()
        sc2[d] = packed[...]

    up_copy.wait()

    def spread_rows(inv):
        for sec in range(SECTIONS):
            inv_b[sec] = jnp.broadcast_to(inv[:, sec:sec + 1], (TOK, 128))

    def find_upper():
        spread_rows(inv_own[...])

        def up_one(t, _):
            rows = pl.ds(pl.multiple_of(t * 32, 32), 32)
            taps = run_sections(
                up_in[rows, :].astype(F32), lambda sec: inv_b[sec, rows, :],
                lambda sec: gain_u[sec], lambda sec: mix_u[sec],
            )
            upper[rows, :] = taps[2].astype(F32)
            return 0

        lax.fori_loop(0, 4, up_one, 0)

    pl.when(jnp.logical_not(home))(find_upper)

    for copy in w_copies:
        copy.wait()

    first, second = pl.ds(0, HALF), pl.ds(HALF, HALF)

    def replica_of(parity, n):
        return lax.rem(y + n, 4) * 2 + parity

    def a1_copy(to_y):
        j = to_y * 2 + 1 - zh
        return remote(
            stage.at[j, :, first], in_a1.at[to_y], a1_send.at[to_y], a1_recv.at[to_y], device_id=at(s, pair)
        )

    def b1_copy(to_y, z):
        j = to_y * 2 + z
        return remote(
            stage.at[j, :, second], in_b1.at[y * 2 + z], b1_send.at[j], b1_recv.at[y * 2 + z],
            device_id=at(s, to_y * 2 + zh),
        )

    def a2_copy(to_y):
        return remote(
            out_a2.at[to_y], in_a2.at[y], a2_send.at[to_y], a2_recv.at[y], device_id=at(s, to_y * 2 + zh)
        )

    def b2_copy():
        return remote(out_b2, in_b2, b2_send.at[0], b2_recv.at[0], device_id=at(s, pair))

    def join(j, z):
        to_y = j // 2
        rows = pl.ds(pl.multiple_of(j * TOK, TOK), TOK)
        part = jnp.dot(feat[rows, :], w[...], preferred_element_type=F32)
        stage[j] = part.astype(BF16)

        @pl.when(z == zh)
        def _():
            keep_a[to_y] = part[:, 0:HALF]

        @pl.when(z != zh)
        def _():
            a1_copy(to_y).start()

        @pl.when(to_y == y)
        def _():
            keep_b[z] = part[:, HALF:OUT]

        @pl.when(to_y != y)
        def _():
            b1_copy(to_y, z).start()

    def f_copy(j, part):
        rows = pl.ds(pl.multiple_of(j * TOK + part * 64, 64), 64)
        slot = (j // 2) * 2 + part
        return remote(feat.at[rows], feat.at[rows], f_send.at[slot], f_recv.at[slot], device_id=at(sib, d))

    def join_other(n):
        j = replica_of(1 - c, n)
        f_copy(j, 0).wait_recv()
        f_copy(j, 1).wait_recv()
        join(j, 1 - c)

    def work(n, _):
        j = replica_of(c, n)
        slot = j // 2
        remote(
            stream.at[:, pl.ds(0, IN)], h0.at[slot], h_send.at[0], h_recv.at[slot], device_id=at(sib, d)
        ).wait_recv()

        @pl.when(j != d)
        def _():
            remote(packed, sc2.at[j], r2_send.at[0], r2_recv.at[j], device_id=at(sib, d)).wait_recv()

        spread_rows(jnp.concatenate([sc2[j], jnp.zeros((128 - SECTIONS, 128), F32)], 0).T)

        def one(t, _):
            rows = pl.ds(pl.multiple_of(t * 16, 16), 16)
            taps = run_sections(
                h0[slot, rows, :].astype(F32), lambda sec: inv_b[sec, rows, :],
                lambda sec: gain_b[sec], lambda sec: mix_b[sec],
            )
            for i, tap in enumerate(taps):
                feat[pl.ds(pl.multiple_of(j * TOK + t * 16, 16), 16), i * IN:(i + 1) * IN] = tap
            return 0

        lax.fori_loop(0, 4, one, 0)
        f_copy(j, 0).start()
        lax.fori_loop(4, 8, one, 0)
        f_copy(j, 1).start()
        join(j, c)

        @pl.when(n > 0)
        def _():
            join_other(n - 1)

        return 0

    lax.fori_loop(0, 4, work, 0)
    join_other(3)

    pl.when(home)(find_upper)

    def turn_out(t):
        rows = pl.ds(pl.multiple_of(t * 512, 512), 512)
        return pltpu.make_async_copy(feat_t.at[rows], feat_out.at[rows], o_sem.at[t])

    def turn(t, _):
        cols = pl.ds(pl.multiple_of(t * 512, 512), 512)

        def block(j, _):
            rows = pl.ds(pl.multiple_of(j * TOK, TOK), TOK)
            feat_t[cols, rows] = feat[rows, cols].T
            return 0

        lax.fori_loop(0, 8, block, 0)
        turn_out(t).start()
        return 0

    @pl.when(jnp.logical_not(home))
    def _():
        lax.fori_loop(0, 2, turn, 0)

    for i in (1, 2, 3, 0):
        to_y = lax.rem(y + i, 4)
        remote(
            stage.at[0, :, first], in_a1.at[to_y], a1_send.at[to_y], a1_recv.at[to_y], device_id=at(s, pair)
        ).wait_recv()
        total = keep_a[to_y] + in_a1[to_y].astype(F32)
        if i > 0:
            out_a2[to_y] = total.astype(BF16)
            post(a2_copy(to_y))
        else:
            own[:, 0:HALF] = total

    for step in range(2):
        z = 1 - zh if step == 0 else zh
        total = keep_b[z]
        for from_y in y_peers:
            slot = from_y * 2 + z
            remote(
                stage.at[0, :, second], in_b1.at[slot], b1_send.at[slot], b1_recv.at[slot],
                device_id=at(s, from_y * 2 + zh),
            ).wait_recv()
            total = total + in_b1[slot].astype(F32)
        if step == 0:
            out_b2[...] = total.astype(BF16)
            post(b2_copy())
        else:
            own[:, HALF:OUT] = total

    @pl.when(home)
    def _():
        lax.fori_loop(0, 2, turn, 0)

    lax.fori_loop(2, 4, turn, 0)

    inv_count = []
    for k in range(1, STEPS + 1):
        count = jnp.int32(0)
        for m in range(NMB):
            count = count + jnp.maximum(lengths[0, m] - k, 0)
        inv_count.append(1.0 / (jnp.full((1, 128), jnp.maximum(count, 1), jnp.int32).astype(F32) * D))

    here = pl.ds(pl.multiple_of(d * TOK, TOK), TOK)

    def draft(q, _):
        cols = pl.ds(pl.multiple_of(q * 128, 128), 128)
        joined = own[:, cols]
        up = upper[:, cols]
        dec = decay[:, cols]
        plen = left[...]

        def carry_of(k):
            return dec * mask_t[:, k - 1:k]

        state = joined
        pulls = []
        for k in range(1, STEPS + 1):
            state = joined + carry_of(k) * pltpu.roll(state, 1, 0)
            target = pltpu.roll(up, TOK - k, 0)
            diff = jnp.where(plen > k, state - target, 0.0)
            loss_acc[k - 1] += jnp.sum((diff * diff).reshape(TOK // 8, 8, 128), axis=0)
            pulls.append(diff * (2.0 * inv_count[k - 1]))
        back = pulls[STEPS - 1]
        total = back
        for k in range(STEPS - 1, 0, -1):
            back = pulls[k - 1] + pltpu.roll(carry_of(k + 1) * back, TOK - 1, 0)
            total = total + back
        total = total + pltpu.roll(carry_of(1) * back, TOK - 1, 0)
        rows_all[here, cols] = total.astype(BF16)
        return 0

    def rows_of(j):
        return pl.ds(pl.multiple_of(j * TOK, TOK), TOK)

    def q_copy(part, i, source, peer):
        block = rows_all.at[rows_of(source), first if part == 0 else second]
        return remote(block, block, q_send.at[part * 4 + i], q_recv.at[part * DP + source], device_id=at(s, peer))

    def qa_copy(i, from_y, to_y):
        block = rows_all.at[rows_of(from_y * 2 + 1 - zh), first]
        return remote(block, block, qa_send.at[i], qa_recv.at[from_y], device_id=at(s, to_y * 2 + zh))

    def qb_copy(i, from_y, z):
        block = rows_all.at[rows_of(from_y * 2 + z), second]
        return remote(block, block, qb_send.at[i], qb_recv.at[from_y], device_id=at(s, pair))

    for i, from_y in enumerate(y_peers):
        remote(
            out_a2.at[0], in_a2.at[from_y], a2_send.at[0], a2_recv.at[from_y], device_id=at(s, from_y * 2 + zh)
        ).wait_recv()
        own[:, 0:HALF] += in_a2[from_y].astype(F32)
    lax.fori_loop(0, 2, draft, 0)
    for i, peer in enumerate([pair] + [p * 2 + zh for p in y_peers]):
        post(q_copy(0, i, d, peer))
    b2_copy().wait_recv()
    own[:, HALF:OUT] += in_b2[...].astype(F32)
    lax.fori_loop(2, 4, draft, 0)
    for i, peer in enumerate([pair] + [p * 2 + zh for p in y_peers]):
        post(q_copy(1, i, d, peer))

    lax.fori_loop(4, 5, turn, 0)
    q_copy(0, 0, pair, pair).wait_recv()
    for i, to_y in enumerate(y_peers):
        post(qa_copy(i, y, to_y))

    lax.fori_loop(5, 6, turn, 0)
    for i, from_y in enumerate(y_peers):
        q_copy(1, 0, from_y * 2 + zh, pair).wait_recv()
        post(qb_copy(i, from_y, zh))

    lane = lax.broadcasted_iota(jnp.int32, (8, 128), 1)
    losses = jnp.zeros((8, 128), F32)
    for k in range(1, STEPS + 1):
        losses = jnp.where(lane == k - 1, jnp.sum(loss_acc[k - 1]) * inv_count[k - 1], losses)
    loss_tile[...] = losses
    loss_all[s] = losses
    for i, peer in enumerate(seg_peers):
        post(remote(loss_tile, loss_all.at[s], l_send.at[i], l_recv.at[s], device_id=at(peer, d)))

    for i, peer in enumerate(seg_peers):
        remote(loss_tile, loss_all.at[peer], l_send.at[i], l_recv.at[peer], device_id=at(peer, d)).wait_recv()
    summed = loss_all[0]
    for i in range(1, SEG):
        summed = summed + loss_all[i]
    loss_out[...] = summed

    q_copy(1, 0, pair, pair).wait_recv()
    for from_y in y_peers:
        q_copy(0, 0, from_y * 2 + zh, pair).wait_recv()
        qa_copy(0, from_y, from_y).wait_recv()
        qb_copy(0, from_y, 1 - zh).wait_recv()
    rows_copy = pltpu.make_async_copy(rows_all, rows_out, in_sem.at[0])
    rows_copy.start()

    for copy in sends:
        copy.wait_send()

    @pl.when(home)
    def _():
        for i in range(DP - 1):
            h_copy(i).wait_send()
            r2_copy(i).wait_send()

    for n in range(4):
        for part in range(2):
            f_copy(replica_of(c, n), part).wait_send()
    for to_y in range(4):
        a1_copy(to_y).wait_send()
    for to_y in y_peers:
        for z in range(2):
            b1_copy(to_y, z).wait_send()
    for t in range(6):
        turn_out(t).wait()
    rows_copy.wait()


def gradient(feat_in, rows_in, loss_in, grad_out, loss_out, feat_t, rows, loss, grad, i_sem, sem):
    def block(t):
        return pl.ds(pl.multiple_of(t * 512, 512), 512)

    def in_copy(t):
        return pltpu.make_async_copy(feat_in.at[block(t)], feat_t.at[block(t)], i_sem.at[t])

    def out_copy(t):
        return pltpu.make_async_copy(grad.at[t], grad_out.at[block(t)], sem.at[t])

    rows_copy = pltpu.make_async_copy(rows_in, rows, i_sem.at[6])
    loss_copy = pltpu.make_async_copy(loss_in, loss, i_sem.at[7])
    rows_copy.start()
    for t in range(6):
        in_copy(t).start()
    loss_copy.start()
    rows_copy.wait()

    def one(t, _):
        in_copy(t).wait()
        grad[t] = jnp.dot(feat_t[block(t), :], rows[...], preferred_element_type=F32)
        out_copy(t).start()
        return 0

    lax.fori_loop(0, 6, one, 0)
    loss_copy.wait()
    loss_out[...] = loss[0:1, 0:STEPS]
    for t in range(6):
        out_copy(t).wait()


def local(stream_in, sec_gain, sec_mix, fc_weight, decay, lengths, ttt_mask):
    vmem = pltpu.VMEM
    dma = pltpu.SemaphoreType.DMA
    scratch = [
        vmem((1, OUT), F32), pltpu.SMEM((1, NMB), jnp.int32), vmem((STEPS, TOK), jnp.int32),
        vmem((SECTIONS, 2, 1, D), F32),
        vmem((SECTIONS, 8, IN), F32), vmem((SECTIONS, 8, IN), F32),
        vmem((SECTIONS, 8, OUT), F32), vmem((SECTIONS, 8, OUT), F32),
        vmem((16, D), BF16), vmem((16, D), F32),
        vmem((4, TOK, IN), BF16),
        vmem((OWN, 128), F32), vmem((SEG, OWN, 128), F32),
        vmem((SECTIONS, 128), F32), vmem((DP, SECTIONS, 128), F32),
        vmem((TOK, 128), F32), vmem((SECTIONS, TOK, 128), F32),
        vmem((3 * IN, OUT), BF16),
        vmem((DP * TOK, 3 * IN), BF16), vmem((3 * IN, DP * TOK), BF16),
        vmem((DP, TOK, OUT), BF16), vmem((4, TOK, HALF), F32), vmem((2, TOK, HALF), F32),
        vmem((4, TOK, HALF), BF16), vmem((DP, TOK, HALF), BF16),
        vmem((4, TOK, HALF), BF16), vmem((4, TOK, HALF), BF16),
        vmem((TOK, HALF), BF16), vmem((TOK, HALF), BF16), vmem((TOK, OUT), F32),
        vmem((TOK, OUT), BF16), vmem((TOK, OUT), F32),
        vmem((TOK, 128), F32), vmem((TOK, 128), F32), vmem((TOK, 128), jnp.int32),
        vmem((STEPS, 8, 128), F32), vmem((8, 128), F32), vmem((SEG, 8, 128), F32),
        vmem((DP * TOK, OUT), BF16),
        dma((10,)), dma((5,)), dma((SEG,)), dma((10,)), dma((DP,)), dma((4,)),
        dma((SEG,)), dma((SEG,)), dma((DP,)), dma((DP,)), dma((DP,)), dma((DP,)),
        dma((4,)), dma((4,)), dma((DP,)), dma((DP,)), dma((4,)), dma((4,)), dma((1,)), dma((1,)),
        dma((8,)), dma((2 * DP,)), dma((3,)), dma((4,)), dma((3,)), dma((4,)), dma((SEG,)), dma((SEG,)), dma((6,)),
    ]
    in_hbm = pl.BlockSpec(memory_space=pltpu.HBM)
    in_vmem = pl.BlockSpec(memory_space=pltpu.VMEM)
    loss, feat_t, rows = pl.pallas_call(
        kernel,
        out_shape=(
            jax.ShapeDtypeStruct((8, 128), F32),
            jax.ShapeDtypeStruct((3 * IN, DP * TOK), BF16),
            jax.ShapeDtypeStruct((DP * TOK, OUT), BF16),
        ),
        in_specs=[in_hbm] * 7,
        out_specs=(in_vmem, in_hbm, in_hbm),
        scratch_shapes=scratch,
        compiler_params=pltpu.CompilerParams(
            collective_id=0, has_side_effects=True, vmem_limit_bytes=VM1 * 1024 * 1024
        ),
        name="window",
    )(stream_in, sec_gain, sec_mix, fc_weight, decay.reshape(1, OUT), lengths, ttt_mask)
    grad, step_loss = pl.pallas_call(
        gradient,
        out_shape=(
            jax.ShapeDtypeStruct((3 * IN, OUT), F32),
            jax.ShapeDtypeStruct((1, STEPS), F32),
        ),
        in_specs=[in_hbm] * 3,
        out_specs=(in_hbm, in_vmem),
        scratch_shapes=[
            vmem((3 * IN, DP * TOK), BF16), vmem((DP * TOK, OUT), BF16), vmem((8, 128), F32),
            vmem((6, 512, OUT), F32), dma((8,)), dma((6,)),
        ],
        compiler_params=pltpu.CompilerParams(vmem_limit_bytes=VM2 * 1024 * 1024),
        name="gradient",
    )(feat_t, rows, loss)
    return step_loss, grad.reshape(3, IN, OUT)


def solution(mesh):
    in_specs = (
        P("dp", None),
        P("segment", None),
        P("segment", None),
        P(None, "dp", "segment"),
        P("segment"),
        P("dp", None),
        P(None, "dp"),
    )
    out_specs = (P("dp", None), P(None, "dp", "segment"))
    return jax.shard_map(local, mesh=mesh, in_specs=in_specs, out_specs=out_specs, check_vma=False)
```

```python
import functools

import jax
import jax.numpy as jnp
from jax import lax
from jax.experimental import pallas as pl
from jax.experimental.pallas import tpu as pltpu
from jax.sharding import PartitionSpec as P

D = 8192
MB = 16
NMB = 8
STEPS = 7
SECTIONS = 16
TAPS = (0, SECTIONS // 2, SECTIONS - 1)
TOK = 128
SEG = 16
DP = 8
CHUNK = 768
VM1 = 47
VM2 = 46
IN = D // DP
OUT = D // SEG
OWN = TOK // SEG
HALF = OUT // 2
F32 = jnp.float32
BF16 = jnp.bfloat16
MESH = pl.DeviceIdType.MESH


def at(segment, dp):
    return {"segment": segment, "dp": dp}


def advance(h, half_gain, mix, inv):
    u = (h * half_gain) * inv
    return (h + (mix * u) * (1.0 + jnp.tanh(u))).astype(BF16)


def run_sections(h, inv_of, gain_of, mix_of):
    rows, cols = h.shape
    taps = []
    for sec in range(SECTIONS):
        gain = jnp.concatenate([gain_of(sec)] * (rows // 8), 0)
        mix = jnp.concatenate([mix_of(sec)] * (rows // 8), 0)
        out = advance(h, gain, mix, jnp.concatenate([inv_of(sec)] * (cols // 128), 1))
        if sec in TAPS:
            taps.append(out)
        h = out.astype(F32)
    return taps


def kernel(stream, gain, mix, weight, decay_in, lengths_in, mask_in, loss_out, feat_t, rows_out,
           decay, lengths, mask, params, gain_b, mix_b, gain_u, mix_u, rows16, hx, h0, tile, sc1, packed, sc2, inv_own, inv_b,
           w, feat, stage, keep_a, keep_b, in_a1, in_b1, out_a2, in_a2, out_b2, in_b2, own,
           up_in, upper, mask_t, mask_pad, left, loss_acc, loss_tile, loss_all, rows_all,
           in_sem, g_send, g_recv, gf_send, h_send, h_recv, r1_send, r1_recv, r2_send, r2_recv, f_send, f_recv,
           a1_send, a1_recv, b1_send, b1_recv, a2_send, a2_recv, b2_send, b2_recv,
           q_send, q_recv, qa_send, qa_recv, qb_send, qb_recv, l_send, l_recv):
    s = lax.axis_index("segment")
    d = lax.axis_index("dp")
    c = lax.rem(s, 2)
    y = d // 2
    zh = lax.rem(d, 2)
    pair = d + 1 - 2 * zh
    sib = s + 1 - 2 * c
    home = zh == c
    seg_peers = [lax.rem(s + i, SEG) for i in range(1, SEG)]
    y_peers = [lax.rem(y + i, 4) for i in range(1, 4)]
    plane = (s // 8) * 8
    x_peers = [plane + lax.rem(s - plane + 2 * i, 8) for i in range(1, 4)]
    across = lax.rem(s + 8, SEG)
    far = [(s, p * 2 + zh) for p in y_peers]
    far = [(across, lax.rem(y + i, 4) * 2 + 1 - zh) for i in (2, 1, 3, 0)] + far
    remote = functools.partial(pltpu.make_async_remote_copy, device_id_type=MESH)

    gain_copy = pltpu.make_async_copy(gain, params.at[s, 0], in_sem.at[5])
    mix_copy = pltpu.make_async_copy(mix, params.at[s, 1], in_sem.at[6])
    gain_copy.start()
    mix_copy.start()
    w_copies = [
        pltpu.make_async_copy(weight.at[i], w.at[pl.ds(i * IN, IN)], in_sem.at[i]) for i in range(3)
    ]
    row0 = pl.multiple_of((s // 2) * 16, 16)
    rows_copy = pltpu.make_async_copy(stream.at[pl.ds(row0, 16)], rows16, in_sem.at[3])
    up_copy = pltpu.make_async_copy(
        stream.at[:, pl.ds(pl.multiple_of(s * OUT, OUT), OUT)], up_in, in_sem.at[4]
    )
    small = [
        pltpu.make_async_copy(src, dst, in_sem.at[7 + i])
        for i, (src, dst) in enumerate(((decay_in, decay), (lengths_in, lengths), (mask_in, mask)))
    ]
    rows_copy.start()
    for copy in small:
        copy.start()

    barrier = pltpu.get_barrier_semaphore()
    for peer in [across, sib] + x_peers:
        pl.semaphore_signal(barrier, inc=1, device_id=at(peer, d), device_id_type=MESH)
    for seg, peer in far + [(s, pair)]:
        pl.semaphore_signal(barrier, inc=1, device_id=at(seg, peer), device_id_type=MESH)
    gain_copy.wait()
    mix_copy.wait()
    pl.semaphore_wait(barrier, 5 + DP)

    def g_copy(slot, peer, send):
        return remote(params.at[slot], params.at[slot], send, g_recv.at[slot], device_id=at(peer, d))

    sends = []

    def post(copy):
        copy.start()
        sends.append(copy)

    for i, peer in enumerate([across] + x_peers + [sib]):
        post(g_copy(s, peer, g_send.at[i]))

    def h_copy(i):
        seg, peer = far[i]
        return remote(
            stream.at[:, pl.ds(pl.multiple_of(peer * IN, IN), IN)], h0.at[y],
            h_send.at[i], h_recv.at[y], device_id=at(seg, peer),
        )

    @pl.when(home)
    def _():
        for i in range(DP - 1):
            h_copy(i).start()
        pltpu.make_async_copy(
            stream.at[:, pl.ds(pl.multiple_of(d * IN, IN), IN)], h0.at[y], h_recv.at[y]
        ).start()

    up_copy.start()
    for copy in w_copies:
        copy.start()

    def wait_param(slot):
        g_copy(slot, sib, g_send.at[0]).wait_recv()

    wait_param(across)
    for i, peer in enumerate(x_peers + [sib]):
        post(g_copy(across, peer, gf_send.at[i]))

    for copy in small:
        copy.wait()
    token = lax.broadcasted_iota(jnp.int32, (TOK, 128), 0)
    pos = token & (MB - 1)
    micro = lax.shift_right_logical(token, 4)
    tok_len = jnp.zeros((TOK, 128), jnp.int32)
    for m in range(NMB):
        tok_len = jnp.where(micro == m, lengths[0, m], tok_len)
    left[...] = tok_len - pos
    mask_pad[...] = jnp.zeros_like(mask_pad)
    mask_pad[0:STEPS, :] = mask[...].astype(F32)
    mask_t[...] = jnp.where(pos >= 1, mask_pad[...].T, 0.0)
    loss_acc[...] = jnp.zeros_like(loss_acc)
    rows_copy.wait()
    hx[...] = rows16[...].astype(F32)

    for i, slot in enumerate(x_peers):
        wait_param(slot)
        post(g_copy(slot, sib, gf_send.at[4 + i]))
    for i, peer in enumerate(x_peers):
        slot = lax.rem(peer + 8, SEG)
        wait_param(slot)
        post(g_copy(slot, sib, gf_send.at[7 + i]))
    for i in range(SEG // 2):
        wait_param(lax.rem(sib + 2 * i, SEG))

    half = pl.ds(pl.multiple_of(c * OWN, OWN), OWN)
    lane = lax.broadcasted_iota(jnp.int32, (OWN, 128), 1)

    def inverse(h):
        return lax.rsqrt(jnp.sum(h * h, axis=1, keepdims=True) * (1.0 / D) + 1e-05)

    def scale_step(sec, carry):
        inv, acc = carry
        acc = jnp.where(lane == sec, inv, acc)
        h = advance(hx[half, :], 0.5 * params[sec, 0], params[sec, 1], inv).astype(F32)
        hx[half, :] = h
        return inverse(h), acc

    inv, acc = lax.fori_loop(
        0, SECTIONS - 1, scale_step, (inverse(hx[half, :]), jnp.zeros((OWN, 128), F32))
    )
    tile[...] = jnp.where(lane == SECTIONS - 1, inv, acc)
    sc1[s] = tile[...]
    chips = [lax.rem(s // 2 + i, SEG // 2) * 2 for i in range(1, SEG // 2)]
    for i, peer in enumerate([p + zh for p in chips] + [sib] + [p + 1 - zh for p in chips]):
        post(remote(tile, sc1.at[s], r1_send.at[i], r1_recv.at[s], device_id=at(peer, d)))

    def spread(sec, _):
        mine = pl.ds(pl.multiple_of(d * IN, IN), IN)
        loss_cols = pl.ds(pl.multiple_of(s * OUT, OUT), OUT)
        gain_b[sec] = jnp.broadcast_to(0.5 * params[sec, 0, :, mine], (8, IN))
        mix_b[sec] = jnp.broadcast_to(params[sec, 1, :, mine], (8, IN))
        gain_u[sec] = jnp.broadcast_to(0.5 * params[sec, 0, :, loss_cols], (8, OUT))
        mix_u[sec] = jnp.broadcast_to(params[sec, 1, :, loss_cols], (8, OUT))
        return 0

    lax.fori_loop(0, SECTIONS, spread, 0)
    for i, peer in enumerate(seg_peers):
        remote(tile, sc1.at[peer], r1_send.at[i], r1_recv.at[peer], device_id=at(peer, d)).wait_recv()
    inv_own[...] = sc1[...].reshape(TOK, 128)
    packed[...] = inv_own[...].T[0:SECTIONS, :]

    def r2_copy(i):
        seg, peer = far[i]
        return remote(packed, sc2.at[d], r2_send.at[i], r2_recv.at[d], device_id=at(seg, peer))

    @pl.when(home)
    def _():
        for i in range(DP - 1):
            r2_copy(i).start()
        sc2[d] = packed[...]

    up_copy.wait()

    def spread_rows(inv):
        for sec in range(SECTIONS):
            inv_b[sec] = jnp.broadcast_to(inv[:, sec:sec + 1], (TOK, 128))

    def find_upper():
        spread_rows(inv_own[...])

        def up_one(t, _):
            rows = pl.ds(pl.multiple_of(t * 32, 32), 32)
            taps = run_sections(
                up_in[rows, :].astype(F32), lambda sec: inv_b[sec, rows, :],
                lambda sec: gain_u[sec], lambda sec: mix_u[sec],
            )
            upper[rows, :] = taps[2].astype(F32)
            return 0

        lax.fori_loop(0, 4, up_one, 0)

    pl.when(jnp.logical_not(home))(find_upper)

    for copy in w_copies:
        copy.wait()

    first, second = pl.ds(0, HALF), pl.ds(HALF, HALF)

    def replica_of(parity, n):
        return lax.rem(y + n, 4) * 2 + parity

    def a1_copy(to_y):
        j = to_y * 2 + 1 - zh
        return remote(
            stage.at[j, :, first], in_a1.at[to_y], a1_send.at[to_y], a1_recv.at[to_y], device_id=at(s, pair)
        )

    def b1_copy(to_y, z):
        j = to_y * 2 + z
        return remote(
            stage.at[j, :, second], in_b1.at[y * 2 + z], b1_send.at[j], b1_recv.at[y * 2 + z],
            device_id=at(s, to_y * 2 + zh),
        )

    def a2_copy(to_y):
        return remote(
            out_a2.at[to_y], in_a2.at[y], a2_send.at[to_y], a2_recv.at[y], device_id=at(s, to_y * 2 + zh)
        )

    def b2_copy():
        return remote(out_b2, in_b2, b2_send.at[0], b2_recv.at[0], device_id=at(s, pair))

    def join(j, z):
        to_y = j // 2
        rows = pl.ds(pl.multiple_of(j * TOK, TOK), TOK)
        part = jnp.dot(feat[rows, :], w[...], preferred_element_type=F32)
        stage[j] = part.astype(BF16)

        @pl.when(z == zh)
        def _():
            keep_a[to_y] = part[:, 0:HALF]

        @pl.when(z != zh)
        def _():
            a1_copy(to_y).start()

        @pl.when(to_y == y)
        def _():
            keep_b[z] = part[:, HALF:OUT]

        @pl.when(to_y != y)
        def _():
            b1_copy(to_y, z).start()

    def f_copy(j, part):
        rows = pl.ds(pl.multiple_of(j * TOK + part * 64, 64), 64)
        slot = (j // 2) * 2 + part
        return remote(feat.at[rows], feat.at[rows], f_send.at[slot], f_recv.at[slot], device_id=at(sib, d))

    def join_other(n):
        j = replica_of(1 - c, n)
        f_copy(j, 0).wait_recv()
        f_copy(j, 1).wait_recv()
        join(j, 1 - c)

    def work(n, _):
        j = replica_of(c, n)
        slot = j // 2
        remote(
            stream.at[:, pl.ds(0, IN)], h0.at[slot], h_send.at[0], h_recv.at[slot], device_id=at(sib, d)
        ).wait_recv()

        @pl.when(j != d)
        def _():
            remote(packed, sc2.at[j], r2_send.at[0], r2_recv.at[j], device_id=at(sib, d)).wait_recv()

        spread_rows(jnp.concatenate([sc2[j], jnp.zeros((128 - SECTIONS, 128), F32)], 0).T)

        def one(t, _):
            rows = pl.ds(pl.multiple_of(t * 16, 16), 16)
            taps = run_sections(
                h0[slot, rows, :].astype(F32), lambda sec: inv_b[sec, rows, :],
                lambda sec: gain_b[sec], lambda sec: mix_b[sec],
            )
            for i, tap in enumerate(taps):
                feat[pl.ds(pl.multiple_of(j * TOK + t * 16, 16), 16), i * IN:(i + 1) * IN] = tap
            return 0

        lax.fori_loop(0, 4, one, 0)
        f_copy(j, 0).start()
        lax.fori_loop(4, 8, one, 0)
        f_copy(j, 1).start()
        join(j, c)

        @pl.when(n > 0)
        def _():
            join_other(n - 1)

        return 0

    lax.fori_loop(0, 4, work, 0)
    join_other(3)

    pl.when(home)(find_upper)

    def turn(t, _):
        cols = pl.ds(pl.multiple_of(t * 512, 512), 512)

        def block(j, _):
            rows = pl.ds(pl.multiple_of(j * TOK, TOK), TOK)
            feat_t[cols, rows] = feat[rows, cols].T
            return 0

        lax.fori_loop(0, 8, block, 0)
        return 0

    @pl.when(jnp.logical_not(home))
    def _():
        lax.fori_loop(0, 2, turn, 0)

    for i in (1, 2, 3, 0):
        to_y = lax.rem(y + i, 4)
        remote(
            stage.at[0, :, first], in_a1.at[to_y], a1_send.at[to_y], a1_recv.at[to_y], device_id=at(s, pair)
        ).wait_recv()
        total = keep_a[to_y] + in_a1[to_y].astype(F32)
        if i > 0:
            out_a2[to_y] = total.astype(BF16)
            post(a2_copy(to_y))
        else:
            own[:, 0:HALF] = total

    for step in range(2):
        z = 1 - zh if step == 0 else zh
        total = keep_b[z]
        for from_y in y_peers:
            slot = from_y * 2 + z
            remote(
                stage.at[0, :, second], in_b1.at[slot], b1_send.at[slot], b1_recv.at[slot],
                device_id=at(s, from_y * 2 + zh),
            ).wait_recv()
            total = total + in_b1[slot].astype(F32)
        if step == 0:
            out_b2[...] = total.astype(BF16)
            post(b2_copy())
        else:
            own[:, HALF:OUT] = total

    @pl.when(home)
    def _():
        lax.fori_loop(0, 2, turn, 0)

    lax.fori_loop(2, 4, turn, 0)

    inv_count = []
    for k in range(1, STEPS + 1):
        count = jnp.int32(0)
        for m in range(NMB):
            count = count + jnp.maximum(lengths[0, m] - k, 0)
        inv_count.append(1.0 / (jnp.full((1, 128), jnp.maximum(count, 1), jnp.int32).astype(F32) * D))

    here = pl.ds(pl.multiple_of(d * TOK, TOK), TOK)

    def draft(q, _):
        cols = pl.ds(pl.multiple_of(q * 128, 128), 128)
        joined = own[:, cols]
        up = upper[:, cols]
        dec = decay[:, cols]
        plen = left[...]

        def carry_of(k):
            return dec * mask_t[:, k - 1:k]

        state = joined
        pulls = []
        for k in range(1, STEPS + 1):
            state = joined + carry_of(k) * pltpu.roll(state, 1, 0)
            target = pltpu.roll(up, TOK - k, 0)
            diff = jnp.where(plen > k, state - target, 0.0)
            loss_acc[k - 1] += jnp.sum((diff * diff).reshape(TOK // 8, 8, 128), axis=0)
            pulls.append(diff * (2.0 * inv_count[k - 1]))
        back = pulls[STEPS - 1]
        total = back
        for k in range(STEPS - 1, 0, -1):
            back = pulls[k - 1] + pltpu.roll(carry_of(k + 1) * back, TOK - 1, 0)
            total = total + back
        total = total + pltpu.roll(carry_of(1) * back, TOK - 1, 0)
        rows_all[here, cols] = total.astype(BF16)
        return 0

    def rows_of(j):
        return pl.ds(pl.multiple_of(j * TOK, TOK), TOK)

    def q_copy(part, i, source, peer):
        block = rows_all.at[rows_of(source), first if part == 0 else second]
        return remote(block, block, q_send.at[part * 4 + i], q_recv.at[part * DP + source], device_id=at(s, peer))

    def qa_copy(i, from_y, to_y):
        block = rows_all.at[rows_of(from_y * 2 + 1 - zh), first]
        return remote(block, block, qa_send.at[i], qa_recv.at[from_y], device_id=at(s, to_y * 2 + zh))

    def qb_copy(i, from_y, z):
        block = rows_all.at[rows_of(from_y * 2 + z), second]
        return remote(block, block, qb_send.at[i], qb_recv.at[from_y], device_id=at(s, pair))

    b2_copy().wait_recv()
    own[:, HALF:OUT] += in_b2[...].astype(F32)
    lax.fori_loop(2, 4, draft, 0)
    over_y = [p * 2 + zh for p in y_peers]
    for i, peer in enumerate(over_y):
        post(q_copy(1, 1 + i, d, peer))
    for i, from_y in enumerate(y_peers):
        remote(
            out_a2.at[0], in_a2.at[from_y], a2_send.at[0], a2_recv.at[from_y], device_id=at(s, from_y * 2 + zh)
        ).wait_recv()
        own[:, 0:HALF] += in_a2[from_y].astype(F32)
    lax.fori_loop(0, 2, draft, 0)
    post(q_copy(0, 0, d, pair))
    lax.fori_loop(4, 5, turn, 0)
    for i, peer in enumerate(over_y):
        post(q_copy(0, 1 + i, d, peer))
    post(q_copy(1, 0, d, pair))
    q_copy(0, 0, pair, pair).wait_recv()
    for i, to_y in enumerate(y_peers):
        post(qa_copy(i, y, to_y))

    lax.fori_loop(5, 6, turn, 0)
    for i, from_y in enumerate(y_peers):
        q_copy(1, 0, from_y * 2 + zh, pair).wait_recv()
        post(qb_copy(i, from_y, zh))

    lane = lax.broadcasted_iota(jnp.int32, (8, 128), 1)
    losses = jnp.zeros((8, 128), F32)
    for k in range(1, STEPS + 1):
        losses = jnp.where(lane == k - 1, jnp.sum(loss_acc[k - 1]) * inv_count[k - 1], losses)
    loss_tile[...] = losses
    loss_all[s] = losses
    for i, peer in enumerate(seg_peers):
        post(remote(loss_tile, loss_all.at[s], l_send.at[i], l_recv.at[s], device_id=at(peer, d)))

    for i, peer in enumerate(seg_peers):
        remote(loss_tile, loss_all.at[peer], l_send.at[i], l_recv.at[peer], device_id=at(peer, d)).wait_recv()
    summed = loss_all[0]
    for i in range(1, SEG):
        summed = summed + loss_all[i]
    loss_out[...] = summed

    q_copy(1, 0, pair, pair).wait_recv()
    for from_y in y_peers:
        q_copy(0, 0, from_y * 2 + zh, pair).wait_recv()
        qa_copy(0, from_y, from_y).wait_recv()
        qb_copy(0, from_y, 1 - zh).wait_recv()
    rows_copy = pltpu.make_async_copy(rows_all, rows_out, in_sem.at[0])
    rows_copy.start()

    for copy in sends:
        copy.wait_send()

    @pl.when(home)
    def _():
        for i in range(DP - 1):
            h_copy(i).wait_send()
            r2_copy(i).wait_send()

    for n in range(4):
        for part in range(2):
            f_copy(replica_of(c, n), part).wait_send()
    for to_y in range(4):
        a1_copy(to_y).wait_send()
    for to_y in y_peers:
        for z in range(2):
            b1_copy(to_y, z).wait_send()
    rows_copy.wait()


def gradient(feat_t, rows, loss, grad_out, loss_out, grad, sem):
    def out_copy(t):
        return pltpu.make_async_copy(grad.at[t], grad_out.at[pl.ds(pl.multiple_of(t * CHUNK, CHUNK), CHUNK)], sem.at[t])

    def one(t, _):
        block = pl.ds(pl.multiple_of(t * CHUNK, CHUNK), CHUNK)
        grad[t] = jnp.dot(feat_t[block, :], rows[...], preferred_element_type=F32)
        out_copy(t).start()
        return 0

    lax.fori_loop(0, 3 * IN // CHUNK, one, 0)
    loss_out[...] = loss[0:1, 0:STEPS]
    for t in range(3 * IN // CHUNK):
        out_copy(t).wait()


def local(stream_in, sec_gain, sec_mix, fc_weight, decay, lengths, ttt_mask):
    vmem = pltpu.VMEM
    dma = pltpu.SemaphoreType.DMA
    scratch = [
        vmem((1, OUT), F32), pltpu.SMEM((1, NMB), jnp.int32), vmem((STEPS, TOK), jnp.int32),
        vmem((SECTIONS, 2, 1, D), F32),
        vmem((SECTIONS, 8, IN), F32), vmem((SECTIONS, 8, IN), F32),
        vmem((SECTIONS, 8, OUT), F32), vmem((SECTIONS, 8, OUT), F32),
        vmem((16, D), BF16), vmem((16, D), F32),
        vmem((4, TOK, IN), BF16),
        vmem((OWN, 128), F32), vmem((SEG, OWN, 128), F32),
        vmem((SECTIONS, 128), F32), vmem((DP, SECTIONS, 128), F32),
        vmem((TOK, 128), F32), vmem((SECTIONS, TOK, 128), F32),
        vmem((3 * IN, OUT), BF16),
        vmem((DP * TOK, 3 * IN), BF16),
        vmem((DP, TOK, OUT), BF16), vmem((4, TOK, HALF), F32), vmem((2, TOK, HALF), F32),
        vmem((4, TOK, HALF), BF16), vmem((DP, TOK, HALF), BF16),
        vmem((4, TOK, HALF), BF16), vmem((4, TOK, HALF), BF16),
        vmem((TOK, HALF), BF16), vmem((TOK, HALF), BF16), vmem((TOK, OUT), F32),
        vmem((TOK, OUT), BF16), vmem((TOK, OUT), F32),
        vmem((TOK, 128), F32), vmem((TOK, 128), F32), vmem((TOK, 128), jnp.int32),
        vmem((STEPS, 8, 128), F32), vmem((8, 128), F32), vmem((SEG, 8, 128), F32),
        vmem((DP * TOK, OUT), BF16),
        dma((10,)), dma((5,)), dma((SEG,)), dma((10,)), dma((DP,)), dma((4,)),
        dma((SEG,)), dma((SEG,)), dma((DP,)), dma((DP,)), dma((DP,)), dma((DP,)),
        dma((4,)), dma((4,)), dma((DP,)), dma((DP,)), dma((4,)), dma((4,)), dma((1,)), dma((1,)),
        dma((8,)), dma((2 * DP,)), dma((3,)), dma((4,)), dma((3,)), dma((4,)), dma((SEG,)), dma((SEG,)),
    ]
    in_hbm = pl.BlockSpec(memory_space=pltpu.HBM)
    in_vmem = pl.BlockSpec(memory_space=pltpu.VMEM)
    loss, feat_t, rows = pl.pallas_call(
        kernel,
        out_shape=(
            vmem((8, 128), F32),
            vmem((3 * IN, DP * TOK), BF16),
            vmem((DP * TOK, OUT), BF16),
        ),
        in_specs=[in_hbm] * 7,
        out_specs=(in_vmem, in_vmem, in_vmem),
        scratch_shapes=scratch,
        compiler_params=pltpu.CompilerParams(
            collective_id=0, has_side_effects=True, vmem_limit_bytes=VM1 * 1024 * 1024
        ),
        name="window",
    )(stream_in, sec_gain, sec_mix, fc_weight, decay.reshape(1, OUT), lengths, ttt_mask)
    grad, step_loss = pl.pallas_call(
        gradient,
        out_shape=(
            jax.ShapeDtypeStruct((3 * IN, OUT), F32),
            jax.ShapeDtypeStruct((1, STEPS), F32),
        ),
        in_specs=[in_vmem] * 3,
        out_specs=(in_hbm, in_vmem),
        scratch_shapes=[vmem((3 * IN // CHUNK, CHUNK, OUT), F32), dma((3 * IN // CHUNK,))],
        compiler_params=pltpu.CompilerParams(vmem_limit_bytes=VM2 * 1024 * 1024),
        name="gradient",
    )(feat_t, rows, loss)
    return step_loss, grad.reshape(3, IN, OUT)


def solution(mesh):
    in_specs = (
        P("dp", None),
        P("segment", None),
        P("segment", None),
        P(None, "dp", "segment"),
        P("segment"),
        P("dp", None),
        P(None, "dp"),
    )
    out_specs = (P("dp", None), P(None, "dp", "segment"))
    return jax.shard_map(local, mesh=mesh, in_specs=in_specs, out_specs=out_specs, check_vma=False)
```

```python
import functools

import jax
import jax.numpy as jnp
from jax import lax
from jax.experimental import pallas as pl
from jax.experimental.pallas import tpu as pltpu
from jax.sharding import PartitionSpec as P

D = 8192
MB = 16
NMB = 8
STEPS = 7
SECTIONS = 16
TAPS = (0, SECTIONS // 2, SECTIONS - 1)
TOK = 128
SEG = 16
DP = 8
CHUNK = 768
VM1 = 47
VM2 = 46
IN = D // DP
OUT = D // SEG
OWN = TOK // SEG
HALF = OUT // 2
F32 = jnp.float32
BF16 = jnp.bfloat16
MESH = pl.DeviceIdType.MESH


def at(segment, dp):
    return {"segment": segment, "dp": dp}


def advance(h, half_gain, mix, inv):
    u = (h * half_gain) * inv
    return (h + (mix * u) * (1.0 + jnp.tanh(u))).astype(BF16)


def run_sections(h, inv_of, gain_of, mix_of):
    rows, cols = h.shape
    taps = []
    for sec in range(SECTIONS):
        gain = jnp.concatenate([gain_of(sec)] * (rows // 8), 0)
        mix = jnp.concatenate([mix_of(sec)] * (rows // 8), 0)
        out = advance(h, gain, mix, jnp.concatenate([inv_of(sec)] * (cols // 128), 1))
        if sec in TAPS:
            taps.append(out)
        h = out.astype(F32)
    return taps


def kernel(stream, gain, mix, weight, decay_in, lengths_in, mask_in, loss_out, feat_t, rows_all,
           decay, lengths, mask, params, gain_b, mix_b, gain_u, mix_u, rows16, hx, h0, tile, sc1, packed, sc2, inv_own, inv_b,
           w, feat, stage, keep_a, keep_b, in_a1, in_b1, out_a2, in_a2, out_b2, in_b2, own,
           up_in, upper, mask_t, mask_pad, left, loss_acc, loss_tile, loss_all,
           in_sem, g_send, g_recv, gf_send, h_send, h_recv, r1_send, r1_recv, r2_send, r2_recv, f_send, f_recv,
           a1_send, a1_recv, b1_send, b1_recv, a2_send, a2_recv, b2_send, b2_recv,
           q_send, q_recv, qa_send, qa_recv, qb_send, qb_recv, l_send, l_recv):
    s = lax.axis_index("segment")
    d = lax.axis_index("dp")
    c = lax.rem(s, 2)
    y = d // 2
    zh = lax.rem(d, 2)
    pair = d + 1 - 2 * zh
    sib = s + 1 - 2 * c
    home = zh == c
    seg_peers = [lax.rem(s + i, SEG) for i in range(1, SEG)]
    y_peers = [lax.rem(y + i, 4) for i in range(1, 4)]
    plane = (s // 8) * 8
    x_peers = [plane + lax.rem(s - plane + 2 * i, 8) for i in range(1, 4)]
    across = lax.rem(s + 8, SEG)
    far = [(s, p * 2 + zh) for p in y_peers]
    far = [(across, lax.rem(y + i, 4) * 2 + 1 - zh) for i in (2, 1, 3, 0)] + far
    remote = functools.partial(pltpu.make_async_remote_copy, device_id_type=MESH)

    gain_copy = pltpu.make_async_copy(gain, params.at[s, 0], in_sem.at[5])
    mix_copy = pltpu.make_async_copy(mix, params.at[s, 1], in_sem.at[6])
    gain_copy.start()
    mix_copy.start()
    w_copies = [
        pltpu.make_async_copy(weight.at[i], w.at[pl.ds(i * IN, IN)], in_sem.at[i]) for i in range(3)
    ]
    row0 = pl.multiple_of((s // 2) * 16, 16)
    rows_copy = pltpu.make_async_copy(stream.at[pl.ds(row0, 16)], rows16, in_sem.at[3])
    up_copy = pltpu.make_async_copy(
        stream.at[:, pl.ds(pl.multiple_of(s * OUT, OUT), OUT)], up_in, in_sem.at[4]
    )
    small = [
        pltpu.make_async_copy(src, dst, in_sem.at[7 + i])
        for i, (src, dst) in enumerate(((decay_in, decay), (lengths_in, lengths), (mask_in, mask)))
    ]
    rows_copy.start()
    for copy in small:
        copy.start()

    barrier = pltpu.get_barrier_semaphore()
    for peer in [across, sib] + x_peers:
        pl.semaphore_signal(barrier, inc=1, device_id=at(peer, d), device_id_type=MESH)
    for seg, peer in far + [(s, pair)]:
        pl.semaphore_signal(barrier, inc=1, device_id=at(seg, peer), device_id_type=MESH)
    gain_copy.wait()
    params[s, 0] = 0.5 * params[s, 0]
    mix_copy.wait()
    pl.semaphore_wait(barrier, 5 + DP)

    def g_copy(slot, peer, send):
        return remote(params.at[slot], params.at[slot], send, g_recv.at[slot], device_id=at(peer, d))

    sends = []

    def post(copy):
        copy.start()
        sends.append(copy)

    for i, peer in enumerate([across] + x_peers + [sib]):
        post(g_copy(s, peer, g_send.at[i]))

    def h_copy(i):
        seg, peer = far[i]
        return remote(
            stream.at[:, pl.ds(pl.multiple_of(peer * IN, IN), IN)], h0.at[y],
            h_send.at[i], h_recv.at[y], device_id=at(seg, peer),
        )

    @pl.when(home)
    def _():
        for i in range(DP - 1):
            h_copy(i).start()
        pltpu.make_async_copy(
            stream.at[:, pl.ds(pl.multiple_of(d * IN, IN), IN)], h0.at[y], h_recv.at[y]
        ).start()

    up_copy.start()
    for copy in w_copies:
        copy.start()

    def wait_param(slot):
        g_copy(slot, sib, g_send.at[0]).wait_recv()

    wait_param(across)
    for i, peer in enumerate(x_peers + [sib]):
        post(g_copy(across, peer, gf_send.at[i]))

    for copy in small:
        copy.wait()
    token = lax.broadcasted_iota(jnp.int32, (TOK, 128), 0)
    pos = token & (MB - 1)
    micro = lax.shift_right_logical(token, 4)
    tok_len = jnp.zeros((TOK, 128), jnp.int32)
    for m in range(NMB):
        tok_len = jnp.where(micro == m, lengths[0, m], tok_len)
    left[...] = tok_len - pos
    mask_pad[...] = jnp.zeros_like(mask_pad)
    mask_pad[0:STEPS, :] = mask[...].astype(F32)
    mask_t[...] = jnp.where(pos >= 1, mask_pad[...].T, 0.0)
    loss_acc[...] = jnp.zeros_like(loss_acc)
    rows_copy.wait()
    hx[...] = rows16[...].astype(F32)

    for i, slot in enumerate(x_peers):
        wait_param(slot)
        post(g_copy(slot, sib, gf_send.at[4 + i]))
    for i, peer in enumerate(x_peers):
        slot = lax.rem(peer + 8, SEG)
        wait_param(slot)
        post(g_copy(slot, sib, gf_send.at[7 + i]))
    for i in range(SEG // 2):
        wait_param(lax.rem(sib + 2 * i, SEG))

    half = pl.ds(pl.multiple_of(c * OWN, OWN), OWN)
    lane = lax.broadcasted_iota(jnp.int32, (OWN, 128), 1)

    def inverse(h):
        return lax.rsqrt(jnp.sum(h * h, axis=1, keepdims=True) * (1.0 / D) + 1e-05)

    def scale_step(sec, carry):
        inv, acc = carry
        acc = jnp.where(lane == sec, inv, acc)
        h = advance(hx[half, :], params[sec, 0], params[sec, 1], inv).astype(F32)
        hx[half, :] = h
        return inverse(h), acc

    inv, acc = lax.fori_loop(
        0, SECTIONS - 1, scale_step, (inverse(hx[half, :]), jnp.zeros((OWN, 128), F32)), unroll=5
    )
    tile[...] = jnp.where(lane == SECTIONS - 1, inv, acc)
    sc1[s] = tile[...]
    chips = [lax.rem(s // 2 + i, SEG // 2) * 2 for i in range(1, SEG // 2)]
    for i, peer in enumerate([p + zh for p in chips] + [sib] + [p + 1 - zh for p in chips]):
        post(remote(tile, sc1.at[s], r1_send.at[i], r1_recv.at[s], device_id=at(peer, d)))

    def spread(sec, _):
        mine = pl.ds(pl.multiple_of(d * IN, IN), IN)
        loss_cols = pl.ds(pl.multiple_of(s * OUT, OUT), OUT)
        gain_b[sec] = jnp.broadcast_to(params[sec, 0, :, mine], (8, IN))
        mix_b[sec] = jnp.broadcast_to(params[sec, 1, :, mine], (8, IN))
        gain_u[sec] = jnp.broadcast_to(params[sec, 0, :, loss_cols], (8, OUT))
        mix_u[sec] = jnp.broadcast_to(params[sec, 1, :, loss_cols], (8, OUT))
        return 0

    lax.fori_loop(0, SECTIONS, spread, 0)
    for i, peer in enumerate(seg_peers):
        remote(tile, sc1.at[peer], r1_send.at[i], r1_recv.at[peer], device_id=at(peer, d)).wait_recv()
    inv_own[...] = sc1[...].reshape(TOK, 128)
    packed[...] = inv_own[...].T[0:SECTIONS, :]

    def r2_copy(i):
        seg, peer = far[i]
        return remote(packed, sc2.at[d], r2_send.at[i], r2_recv.at[d], device_id=at(seg, peer))

    @pl.when(home)
    def _():
        for i in range(DP - 1):
            r2_copy(i).start()
        sc2[d] = packed[...]

    up_copy.wait()

    def spread_rows(inv):
        for sec in range(SECTIONS):
            inv_b[sec] = jnp.broadcast_to(inv[:, sec:sec + 1], (TOK, 128))

    def find_upper():
        spread_rows(inv_own[...])

        def up_one(t, _):
            rows = pl.ds(pl.multiple_of(t * 32, 32), 32)
            taps = run_sections(
                up_in[rows, :].astype(F32), lambda sec: inv_b[sec, rows, :],
                lambda sec: gain_u[sec], lambda sec: mix_u[sec],
            )
            upper[rows, :] = taps[2].astype(F32)
            return 0

        lax.fori_loop(0, 4, up_one, 0)

    pl.when(jnp.logical_not(home))(find_upper)

    for copy in w_copies:
        copy.wait()

    first, second = pl.ds(0, HALF), pl.ds(HALF, HALF)

    def replica_of(parity, n):
        return lax.rem(y + n, 4) * 2 + parity

    def a1_copy(to_y):
        j = to_y * 2 + 1 - zh
        return remote(
            stage.at[j, :, first], in_a1.at[to_y], a1_send.at[to_y], a1_recv.at[to_y], device_id=at(s, pair)
        )

    def b1_copy(to_y, z):
        j = to_y * 2 + z
        return remote(
            stage.at[j, :, second], in_b1.at[y * 2 + z], b1_send.at[j], b1_recv.at[y * 2 + z],
            device_id=at(s, to_y * 2 + zh),
        )

    def a2_copy(to_y):
        return remote(
            out_a2.at[to_y], in_a2.at[y], a2_send.at[to_y], a2_recv.at[y], device_id=at(s, to_y * 2 + zh)
        )

    def b2_copy():
        return remote(out_b2, in_b2, b2_send.at[0], b2_recv.at[0], device_id=at(s, pair))

    def give(j, z, part):
        to_y = j // 2
        stage[j] = part.astype(BF16)

        @pl.when(z == zh)
        def _():
            keep_a[to_y] = part[:, 0:HALF]

        @pl.when(z != zh)
        def _():
            a1_copy(to_y).start()

        @pl.when(to_y == y)
        def _():
            keep_b[z] = part[:, HALF:OUT]

        @pl.when(to_y != y)
        def _():
            b1_copy(to_y, z).start()

    def f_copy(j, part):
        rows = pl.ds(pl.multiple_of(j * TOK + part * 64, 64), 64)
        slot = (j // 2) * 2 + part
        return remote(feat.at[rows], feat.at[rows], f_send.at[slot], f_recv.at[slot], device_id=at(sib, d))

    def join(n):
        to_y = lax.rem(y + n, 4)
        for part in range(2):
            f_copy(to_y * 2 + 1 - c, part).wait_recv()
        rows = pl.ds(pl.multiple_of(to_y * 2 * TOK, 2 * TOK), 2 * TOK)
        both = jnp.dot(feat[rows, :], w[...], preferred_element_type=F32)
        for z in range(2):
            give(to_y * 2 + z, z, both[z * TOK:(z + 1) * TOK, :])

    def work(n, _):
        j = replica_of(c, n)
        slot = j // 2
        remote(
            stream.at[:, pl.ds(0, IN)], h0.at[slot], h_send.at[0], h_recv.at[slot], device_id=at(sib, d)
        ).wait_recv()

        @pl.when(j != d)
        def _():
            remote(packed, sc2.at[j], r2_send.at[0], r2_recv.at[j], device_id=at(sib, d)).wait_recv()

        spread_rows(jnp.concatenate([sc2[j], jnp.zeros((128 - SECTIONS, 128), F32)], 0).T)

        def one(t, _):
            rows = pl.ds(pl.multiple_of(t * 16, 16), 16)
            taps = run_sections(
                h0[slot, rows, :].astype(F32), lambda sec: inv_b[sec, rows, :],
                lambda sec: gain_b[sec], lambda sec: mix_b[sec],
            )
            for i, tap in enumerate(taps):
                feat[pl.ds(pl.multiple_of(j * TOK + t * 16, 16), 16), i * IN:(i + 1) * IN] = tap
            return 0

        lax.fori_loop(0, 4, one, 0)
        f_copy(j, 0).start()
        lax.fori_loop(4, 8, one, 0)
        f_copy(j, 1).start()

        @pl.when(n > 0)
        def _():
            join(n - 1)

        return 0

    lax.fori_loop(0, 4, work, 0)

    last = lax.rem(y + 3, 4) * 2

    def last_one(z):
        j = last + z
        give(j, z, jnp.dot(feat[pl.ds(pl.multiple_of(j * TOK, TOK), TOK), :], w[...], preferred_element_type=F32))

    last_one(c)
    for part in range(2):
        f_copy(last + 1 - c, part).wait_recv()
    last_one(1 - c)

    pl.when(home)(find_upper)

    def turn(t, _):
        cols = pl.ds(pl.multiple_of(t * 512, 512), 512)

        def block(j, _):
            rows = pl.ds(pl.multiple_of(j * TOK, TOK), TOK)
            feat_t[cols, rows] = feat[rows, cols].T
            return 0

        lax.fori_loop(0, 8, block, 0)
        return 0

    @pl.when(jnp.logical_not(home))
    def _():
        lax.fori_loop(0, 2, turn, 0)

    for i in (1, 2, 3, 0):
        to_y = lax.rem(y + i, 4)
        remote(
            stage.at[0, :, first], in_a1.at[to_y], a1_send.at[to_y], a1_recv.at[to_y], device_id=at(s, pair)
        ).wait_recv()
        total = keep_a[to_y] + in_a1[to_y].astype(F32)
        if i > 0:
            out_a2[to_y] = total.astype(BF16)
            post(a2_copy(to_y))
        else:
            own[:, 0:HALF] = total

    for step in range(2):
        z = 1 - zh if step == 0 else zh
        total = keep_b[z]
        for from_y in y_peers:
            slot = from_y * 2 + z
            remote(
                stage.at[0, :, second], in_b1.at[slot], b1_send.at[slot], b1_recv.at[slot],
                device_id=at(s, from_y * 2 + zh),
            ).wait_recv()
            total = total + in_b1[slot].astype(F32)
        if step == 0:
            out_b2[...] = total.astype(BF16)
            post(b2_copy())
        else:
            own[:, HALF:OUT] = total

    @pl.when(home)
    def _():
        lax.fori_loop(0, 2, turn, 0)

    lax.fori_loop(2, 4, turn, 0)

    inv_count = []
    for k in range(1, STEPS + 1):
        count = jnp.int32(0)
        for m in range(NMB):
            count = count + jnp.maximum(lengths[0, m] - k, 0)
        inv_count.append(1.0 / (jnp.full((1, 128), jnp.maximum(count, 1), jnp.int32).astype(F32) * D))

    here = pl.ds(pl.multiple_of(d * TOK, TOK), TOK)

    def draft(q, _):
        cols = pl.ds(pl.multiple_of(q * 128, 128), 128)
        joined = own[:, cols]
        up = upper[:, cols]
        dec = decay[:, cols]
        plen = left[...]

        def carry_of(k):
            return dec * mask_t[:, k - 1:k]

        state = joined
        pulls = []
        for k in range(1, STEPS + 1):
            state = joined + carry_of(k) * pltpu.roll(state, 1, 0)
            target = pltpu.roll(up, TOK - k, 0)
            diff = jnp.where(plen > k, state - target, 0.0)
            loss_acc[k - 1] += jnp.sum((diff * diff).reshape(TOK // 8, 8, 128), axis=0)
            pulls.append(diff * (2.0 * inv_count[k - 1]))
        back = pulls[STEPS - 1]
        total = back
        for k in range(STEPS - 1, 0, -1):
            back = pulls[k - 1] + pltpu.roll(carry_of(k + 1) * back, TOK - 1, 0)
            total = total + back
        total = total + pltpu.roll(carry_of(1) * back, TOK - 1, 0)
        rows_all[here, cols] = total.astype(BF16)
        return 0

    def rows_of(j):
        return pl.ds(pl.multiple_of(j * TOK, TOK), TOK)

    def q_copy(part, i, source, peer):
        block = rows_all.at[rows_of(source), first if part == 0 else second]
        return remote(block, block, q_send.at[part * 4 + i], q_recv.at[part * DP + source], device_id=at(s, peer))

    def qa_copy(i, from_y, to_y):
        block = rows_all.at[rows_of(from_y * 2 + 1 - zh), first]
        return remote(block, block, qa_send.at[i], qa_recv.at[from_y], device_id=at(s, to_y * 2 + zh))

    def qb_copy(i, from_y, z):
        block = rows_all.at[rows_of(from_y * 2 + z), second]
        return remote(block, block, qb_send.at[i], qb_recv.at[from_y], device_id=at(s, pair))

    early, sends[:] = list(sends), []
    b2_copy().wait_recv()
    own[:, HALF:OUT] += in_b2[...].astype(F32)
    lax.fori_loop(2, 4, draft, 0)
    over_y = [p * 2 + zh for p in y_peers]
    for i, peer in enumerate(over_y):
        post(q_copy(1, 1 + i, d, peer))
    for i, from_y in enumerate(y_peers):
        remote(
            out_a2.at[0], in_a2.at[from_y], a2_send.at[0], a2_recv.at[from_y], device_id=at(s, from_y * 2 + zh)
        ).wait_recv()
        own[:, 0:HALF] += in_a2[from_y].astype(F32)
    lax.fori_loop(0, 2, draft, 0)
    post(q_copy(0, 0, d, pair))
    lax.fori_loop(4, 5, turn, 0)
    for i, peer in enumerate(over_y):
        post(q_copy(0, 1 + i, d, peer))
    post(q_copy(1, 0, d, pair))
    q_copy(0, 0, pair, pair).wait_recv()
    for i, to_y in enumerate(y_peers):
        post(qa_copy(i, y, to_y))

    lax.fori_loop(5, 6, turn, 0)
    for copy in early:
        copy.wait_send()

    @pl.when(home)
    def _():
        for i in range(DP - 1):
            h_copy(i).wait_send()
            r2_copy(i).wait_send()

    for n in range(4):
        for part in range(2):
            f_copy(replica_of(c, n), part).wait_send()
    for to_y in range(4):
        a1_copy(to_y).wait_send()
    for to_y in y_peers:
        for z in range(2):
            b1_copy(to_y, z).wait_send()

    for i, from_y in enumerate(y_peers):
        q_copy(1, 0, from_y * 2 + zh, pair).wait_recv()
        post(qb_copy(i, from_y, zh))

    lane = lax.broadcasted_iota(jnp.int32, (8, 128), 1)
    losses = jnp.zeros((8, 128), F32)
    for k in range(1, STEPS + 1):
        losses = jnp.where(lane == k - 1, jnp.sum(loss_acc[k - 1]) * inv_count[k - 1], losses)
    loss_tile[...] = losses
    loss_all[s] = losses
    for i, peer in enumerate(seg_peers):
        post(remote(loss_tile, loss_all.at[s], l_send.at[i], l_recv.at[s], device_id=at(peer, d)))

    for i, peer in enumerate(seg_peers):
        remote(loss_tile, loss_all.at[peer], l_send.at[i], l_recv.at[peer], device_id=at(peer, d)).wait_recv()
    summed = loss_all[0]
    for i in range(1, SEG):
        summed = summed + loss_all[i]
    loss_out[...] = summed

    q_copy(1, 0, pair, pair).wait_recv()
    for from_y in y_peers:
        q_copy(0, 0, from_y * 2 + zh, pair).wait_recv()
        qa_copy(0, from_y, from_y).wait_recv()
        qb_copy(0, from_y, 1 - zh).wait_recv()

    for copy in sends:
        copy.wait_send()


def gradient(feat_t, rows, loss, grad_out, loss_out, grad, sem):
    def out_copy(t):
        return pltpu.make_async_copy(grad.at[t], grad_out.at[pl.ds(pl.multiple_of(t * CHUNK, CHUNK), CHUNK)], sem.at[t])

    def one(t, _):
        block = pl.ds(pl.multiple_of(t * CHUNK, CHUNK), CHUNK)
        grad[t] = jnp.dot(feat_t[block, :], rows[...], preferred_element_type=F32)
        out_copy(t).start()
        return 0

    lax.fori_loop(0, 3 * IN // CHUNK, one, 0)
    loss_out[...] = loss[0:1, 0:STEPS]
    for t in range(3 * IN // CHUNK):
        out_copy(t).wait()


def local(stream_in, sec_gain, sec_mix, fc_weight, decay, lengths, ttt_mask):
    vmem = pltpu.VMEM
    dma = pltpu.SemaphoreType.DMA
    scratch = [
        vmem((1, OUT), F32), pltpu.SMEM((1, NMB), jnp.int32), vmem((STEPS, TOK), jnp.int32),
        vmem((SECTIONS, 2, 1, D), F32),
        vmem((SECTIONS, 8, IN), F32), vmem((SECTIONS, 8, IN), F32),
        vmem((SECTIONS, 8, OUT), F32), vmem((SECTIONS, 8, OUT), F32),
        vmem((16, D), BF16), vmem((16, D), F32),
        vmem((4, TOK, IN), BF16),
        vmem((OWN, 128), F32), vmem((SEG, OWN, 128), F32),
        vmem((SECTIONS, 128), F32), vmem((DP, SECTIONS, 128), F32),
        vmem((TOK, 128), F32), vmem((SECTIONS, TOK, 128), F32),
        vmem((3 * IN, OUT), BF16),
        vmem((DP * TOK, 3 * IN), BF16),
        vmem((DP, TOK, OUT), BF16), vmem((4, TOK, HALF), F32), vmem((2, TOK, HALF), F32),
        vmem((4, TOK, HALF), BF16), vmem((DP, TOK, HALF), BF16),
        vmem((4, TOK, HALF), BF16), vmem((4, TOK, HALF), BF16),
        vmem((TOK, HALF), BF16), vmem((TOK, HALF), BF16), vmem((TOK, OUT), F32),
        vmem((TOK, OUT), BF16), vmem((TOK, OUT), F32),
        vmem((TOK, 128), F32), vmem((TOK, 128), F32), vmem((TOK, 128), jnp.int32),
        vmem((STEPS, 8, 128), F32), vmem((8, 128), F32), vmem((SEG, 8, 128), F32),
        dma((10,)), dma((5,)), dma((SEG,)), dma((10,)), dma((DP,)), dma((4,)),
        dma((SEG,)), dma((SEG,)), dma((DP,)), dma((DP,)), dma((DP,)), dma((DP,)),
        dma((4,)), dma((4,)), dma((DP,)), dma((DP,)), dma((4,)), dma((4,)), dma((1,)), dma((1,)),
        dma((8,)), dma((2 * DP,)), dma((3,)), dma((4,)), dma((3,)), dma((4,)), dma((SEG,)), dma((SEG,)),
    ]
    in_hbm = pl.BlockSpec(memory_space=pltpu.HBM)
    in_vmem = pl.BlockSpec(memory_space=pltpu.VMEM)
    loss, feat_t, rows = pl.pallas_call(
        kernel,
        out_shape=(
            vmem((8, 128), F32),
            vmem((3 * IN, DP * TOK), BF16),
            vmem((DP * TOK, OUT), BF16),
        ),
        in_specs=[in_hbm] * 7,
        out_specs=(in_vmem, in_vmem, in_vmem),
        scratch_shapes=scratch,
        compiler_params=pltpu.CompilerParams(
            collective_id=0, has_side_effects=True, vmem_limit_bytes=VM1 * 1024 * 1024
        ),
        name="window",
    )(stream_in, sec_gain, sec_mix, fc_weight, decay.reshape(1, OUT), lengths, ttt_mask)
    grad, step_loss = pl.pallas_call(
        gradient,
        out_shape=(
            jax.ShapeDtypeStruct((3 * IN, OUT), F32),
            jax.ShapeDtypeStruct((1, STEPS), F32),
        ),
        in_specs=[in_vmem] * 3,
        out_specs=(in_hbm, in_vmem),
        scratch_shapes=[vmem((3 * IN // CHUNK, CHUNK, OUT), F32), dma((3 * IN // CHUNK,))],
        compiler_params=pltpu.CompilerParams(vmem_limit_bytes=VM2 * 1024 * 1024),
        name="gradient",
    )(feat_t, rows, loss)
    return step_loss, grad.reshape(3, IN, OUT)


def solution(mesh):
    in_specs = (
        P("dp", None),
        P("segment", None),
        P("segment", None),
        P(None, "dp", "segment"),
        P("segment"),
        P("dp", None),
        P(None, "dp"),
    )
    out_specs = (P("dp", None), P(None, "dp", "segment"))
    return jax.shard_map(local, mesh=mesh, in_specs=in_specs, out_specs=out_specs, check_vma=False)
```

```python
import functools

import jax
import jax.numpy as jnp
from jax import lax
from jax.experimental import pallas as pl
from jax.experimental.pallas import tpu as pltpu
from jax.sharding import PartitionSpec as P

D = 8192
MB = 16
NMB = 8
STEPS = 7
SECTIONS = 16
TAPS = (0, SECTIONS // 2, SECTIONS - 1)
TOK = 128
SEG = 16
DP = 8
CHUNK = 1024
VM1 = 47
VM2 = 46
IN = D // DP
OUT = D // SEG
OWN = TOK // SEG
HALF = OUT // 2
F32 = jnp.float32
BF16 = jnp.bfloat16
MESH = pl.DeviceIdType.MESH


def at(segment, dp):
    return {"segment": segment, "dp": dp}


def advance(h, half_gain, mix, inv):
    u = (h * half_gain) * inv
    return (h + (mix * u) * (1.0 + jnp.tanh(u))).astype(BF16)


def run_sections(h, inv_of, gain_of, mix_of):
    rows, cols = h.shape
    taps = []
    for sec in range(SECTIONS):
        gain = jnp.concatenate([gain_of(sec)] * (rows // 8), 0)
        mix = jnp.concatenate([mix_of(sec)] * (rows // 8), 0)
        out = advance(h, gain, mix, jnp.concatenate([inv_of(sec)] * (cols // 128), 1))
        if sec in TAPS:
            taps.append(out)
        h = out.astype(F32)
    return taps


def kernel(stream, gain, mix, weight, decay_in, lengths_in, mask_in, loss_out, feat_t, rows_all,
           decay, lengths, mask, params, gain_b, mix_b, gain_u, mix_u, rows16, hx, h0, tile, sc1, packed, sc2, inv_own, inv_b,
           w, feat, stage, keep_a, keep_b, in_a1, in_b1, out_a2, in_a2, out_b2, in_b2, own,
           up_in, upper, mask_t, mask_pad, left, loss_acc, loss_tile, loss_all,
           in_sem, g_send, g_recv, gf_send, h_send, h_recv, r1_send, r1_recv, r2_send, r2_recv, f_send, f_recv,
           a1_send, a1_recv, b1_send, b1_recv, a2_send, a2_recv, b2_send, b2_recv,
           q_send, q_recv, qa_send, qa_recv, qb_send, qb_recv, l_send, l_recv):
    s = lax.axis_index("segment")
    d = lax.axis_index("dp")
    c = lax.rem(s, 2)
    y = d // 2
    zh = lax.rem(d, 2)
    pair = d + 1 - 2 * zh
    sib = s + 1 - 2 * c
    home = zh == c
    seg_peers = [lax.rem(s + i, SEG) for i in range(1, SEG)]
    y_peers = [lax.rem(y + i, 4) for i in range(1, 4)]
    plane = (s // 8) * 8
    x_peers = [plane + lax.rem(s - plane + 2 * i, 8) for i in range(1, 4)]
    across = lax.rem(s + 8, SEG)
    far = [(s, p * 2 + zh) for p in y_peers]
    far = [(across, lax.rem(y + i, 4) * 2 + 1 - zh) for i in (2, 1, 3, 0)] + far
    remote = functools.partial(pltpu.make_async_remote_copy, device_id_type=MESH)

    gain_copy = pltpu.make_async_copy(gain, params.at[s, 0], in_sem.at[5])
    mix_copy = pltpu.make_async_copy(mix, params.at[s, 1], in_sem.at[6])
    gain_copy.start()
    mix_copy.start()
    w_copies = [
        pltpu.make_async_copy(weight.at[i], w.at[pl.ds(i * IN, IN)], in_sem.at[i]) for i in range(3)
    ]
    row0 = pl.multiple_of((s // 2) * 16, 16)
    rows_copy = pltpu.make_async_copy(stream.at[pl.ds(row0, 16)], rows16, in_sem.at[3])
    up_copy = pltpu.make_async_copy(
        stream.at[:, pl.ds(pl.multiple_of(s * OUT, OUT), OUT)], up_in, in_sem.at[4]
    )
    small = [
        pltpu.make_async_copy(src, dst, in_sem.at[7 + i])
        for i, (src, dst) in enumerate(((decay_in, decay), (lengths_in, lengths), (mask_in, mask)))
    ]
    rows_copy.start()
    for copy in small:
        copy.start()

    barrier = pltpu.get_barrier_semaphore()
    for peer in [across, sib] + x_peers:
        pl.semaphore_signal(barrier, inc=1, device_id=at(peer, d), device_id_type=MESH)
    for seg, peer in far + [(s, pair)]:
        pl.semaphore_signal(barrier, inc=1, device_id=at(seg, peer), device_id_type=MESH)
    gain_copy.wait()
    params[s, 0] = 0.5 * params[s, 0]
    mix_copy.wait()
    pl.semaphore_wait(barrier, 5 + DP)

    def g_copy(slot, peer, send):
        return remote(params.at[slot], params.at[slot], send, g_recv.at[slot], device_id=at(peer, d))

    sends = []

    def post(copy):
        copy.start()
        sends.append(copy)

    for i, peer in enumerate([across] + x_peers + [sib]):
        post(g_copy(s, peer, g_send.at[i]))

    def h_copy(i):
        seg, peer = far[i]
        return remote(
            stream.at[:, pl.ds(pl.multiple_of(peer * IN, IN), IN)], h0.at[y],
            h_send.at[i], h_recv.at[y], device_id=at(seg, peer),
        )

    @pl.when(home)
    def _():
        for i in range(DP - 1):
            h_copy(i).start()
        pltpu.make_async_copy(
            stream.at[:, pl.ds(pl.multiple_of(d * IN, IN), IN)], h0.at[y], h_recv.at[y]
        ).start()

    up_copy.start()
    for copy in w_copies:
        copy.start()

    def wait_param(slot):
        g_copy(slot, sib, g_send.at[0]).wait_recv()

    wait_param(across)
    for i, peer in enumerate(x_peers + [sib]):
        post(g_copy(across, peer, gf_send.at[i]))

    for copy in small:
        copy.wait()
    token = lax.broadcasted_iota(jnp.int32, (TOK, 128), 0)
    pos = token & (MB - 1)
    micro = lax.shift_right_logical(token, 4)
    tok_len = jnp.zeros((TOK, 128), jnp.int32)
    for m in range(NMB):
        tok_len = jnp.where(micro == m, lengths[0, m], tok_len)
    left[...] = tok_len - pos
    mask_pad[...] = jnp.zeros_like(mask_pad)
    mask_pad[0:STEPS, :] = mask[...].astype(F32)
    mask_t[...] = jnp.where(pos >= 1, mask_pad[...].T, 0.0)
    loss_acc[...] = jnp.zeros_like(loss_acc)
    rows_copy.wait()
    hx[...] = rows16[...].astype(F32)

    for i, slot in enumerate(x_peers):
        wait_param(slot)
        post(g_copy(slot, sib, gf_send.at[4 + i]))
    for i, peer in enumerate(x_peers):
        slot = lax.rem(peer + 8, SEG)
        wait_param(slot)
        post(g_copy(slot, sib, gf_send.at[7 + i]))
    for i in range(SEG // 2):
        wait_param(lax.rem(sib + 2 * i, SEG))

    half = pl.ds(pl.multiple_of(c * OWN, OWN), OWN)
    lane = lax.broadcasted_iota(jnp.int32, (OWN, 128), 1)

    def inverse(h):
        return lax.rsqrt(jnp.sum(h * h, axis=1, keepdims=True) * (1.0 / D) + 1e-05)

    def scale_step(sec, carry):
        inv, acc = carry
        acc = jnp.where(lane == sec, inv, acc)
        h = advance(hx[half, :], params[sec, 0], params[sec, 1], inv).astype(F32)
        hx[half, :] = h
        return inverse(h), acc

    inv, acc = lax.fori_loop(
        0, SECTIONS - 1, scale_step, (inverse(hx[half, :]), jnp.zeros((OWN, 128), F32)), unroll=5
    )
    tile[...] = jnp.where(lane == SECTIONS - 1, inv, acc)
    sc1[s] = tile[...]
    chips = [lax.rem(s // 2 + i, SEG // 2) * 2 for i in range(1, SEG // 2)]
    for i, peer in enumerate([p + zh for p in chips] + [sib] + [p + 1 - zh for p in chips]):
        post(remote(tile, sc1.at[s], r1_send.at[i], r1_recv.at[s], device_id=at(peer, d)))

    def spread(sec, _):
        mine = pl.ds(pl.multiple_of(d * IN, IN), IN)
        loss_cols = pl.ds(pl.multiple_of(s * OUT, OUT), OUT)
        gain_b[sec] = jnp.broadcast_to(params[sec, 0, :, mine], (8, IN))
        mix_b[sec] = jnp.broadcast_to(params[sec, 1, :, mine], (8, IN))
        gain_u[sec] = jnp.broadcast_to(params[sec, 0, :, loss_cols], (8, OUT))
        mix_u[sec] = jnp.broadcast_to(params[sec, 1, :, loss_cols], (8, OUT))
        return 0

    lax.fori_loop(0, SECTIONS, spread, 0)
    for i, peer in enumerate(seg_peers):
        remote(tile, sc1.at[peer], r1_send.at[i], r1_recv.at[peer], device_id=at(peer, d)).wait_recv()
    inv_own[...] = sc1[...].reshape(TOK, 128)
    packed[...] = inv_own[...].T[0:SECTIONS, :]

    def r2_copy(i):
        seg, peer = far[i]
        return remote(packed, sc2.at[d], r2_send.at[i], r2_recv.at[d], device_id=at(seg, peer))

    @pl.when(home)
    def _():
        for i in range(DP - 1):
            r2_copy(i).start()
        sc2[d] = packed[...]

    up_copy.wait()

    def spread_rows(inv):
        for sec in range(SECTIONS):
            inv_b[sec] = jnp.broadcast_to(inv[:, sec:sec + 1], (TOK, 128))

    def find_upper():
        spread_rows(inv_own[...])

        def up_one(t, _):
            rows = pl.ds(pl.multiple_of(t * 32, 32), 32)
            taps = run_sections(
                up_in[rows, :].astype(F32), lambda sec: inv_b[sec, rows, :],
                lambda sec: gain_u[sec], lambda sec: mix_u[sec],
            )
            upper[rows, :] = taps[2].astype(F32)
            return 0

        lax.fori_loop(0, 4, up_one, 0)

    pl.when(jnp.logical_not(home))(find_upper)

    for copy in w_copies:
        copy.wait()

    first, second = pl.ds(0, HALF), pl.ds(HALF, HALF)

    def replica_of(parity, n):
        return lax.rem(y + n, 4) * 2 + parity

    def a1_copy(to_y):
        j = to_y * 2 + 1 - zh
        return remote(
            stage.at[j, :, first], in_a1.at[to_y], a1_send.at[to_y], a1_recv.at[to_y], device_id=at(s, pair)
        )

    def b1_copy(to_y, z):
        j = to_y * 2 + z
        return remote(
            stage.at[j, :, second], in_b1.at[y * 2 + z], b1_send.at[j], b1_recv.at[y * 2 + z],
            device_id=at(s, to_y * 2 + zh),
        )

    def a2_copy(to_y):
        return remote(
            out_a2.at[to_y], in_a2.at[y], a2_send.at[to_y], a2_recv.at[y], device_id=at(s, to_y * 2 + zh)
        )

    def b2_copy():
        return remote(out_b2, in_b2, b2_send.at[0], b2_recv.at[0], device_id=at(s, pair))

    def give(j, z, part):
        to_y = j // 2
        stage[j] = part.astype(BF16)

        @pl.when(z == zh)
        def _():
            keep_a[to_y] = part[:, 0:HALF]

        @pl.when(z != zh)
        def _():
            a1_copy(to_y).start()

        @pl.when(to_y == y)
        def _():
            keep_b[z] = part[:, HALF:OUT]

        @pl.when(to_y != y)
        def _():
            b1_copy(to_y, z).start()

    def f_copy(j, part):
        rows = pl.ds(pl.multiple_of(j * TOK + part * 64, 64), 64)
        slot = (j // 2) * 2 + part
        return remote(feat.at[rows], feat.at[rows], f_send.at[slot], f_recv.at[slot], device_id=at(sib, d))

    def join(n):
        to_y = lax.rem(y + n, 4)
        for part in range(2):
            f_copy(to_y * 2 + 1 - c, part).wait_recv()
        rows = pl.ds(pl.multiple_of(to_y * 2 * TOK, 2 * TOK), 2 * TOK)
        both = jnp.dot(feat[rows, :], w[...], preferred_element_type=F32)
        for z in range(2):
            give(to_y * 2 + z, z, both[z * TOK:(z + 1) * TOK, :])

    def work(n, _):
        j = replica_of(c, n)
        slot = j // 2
        remote(
            stream.at[:, pl.ds(0, IN)], h0.at[slot], h_send.at[0], h_recv.at[slot], device_id=at(sib, d)
        ).wait_recv()

        @pl.when(j != d)
        def _():
            remote(packed, sc2.at[j], r2_send.at[0], r2_recv.at[j], device_id=at(sib, d)).wait_recv()

        spread_rows(jnp.concatenate([sc2[j], jnp.zeros((128 - SECTIONS, 128), F32)], 0).T)

        def one(t, _):
            rows = pl.ds(pl.multiple_of(t * 16, 16), 16)
            taps = run_sections(
                h0[slot, rows, :].astype(F32), lambda sec: inv_b[sec, rows, :],
                lambda sec: gain_b[sec], lambda sec: mix_b[sec],
            )
            for i, tap in enumerate(taps):
                feat[pl.ds(pl.multiple_of(j * TOK + t * 16, 16), 16), i * IN:(i + 1) * IN] = tap
            return 0

        lax.fori_loop(0, 4, one, 0)
        f_copy(j, 0).start()
        lax.fori_loop(4, 8, one, 0)
        f_copy(j, 1).start()

        @pl.when(n > 0)
        def _():
            join(n - 1)

        return 0

    lax.fori_loop(0, 4, work, 0)

    last = lax.rem(y + 3, 4) * 2

    def last_one(z):
        j = last + z
        give(j, z, jnp.dot(feat[pl.ds(pl.multiple_of(j * TOK, TOK), TOK), :], w[...], preferred_element_type=F32))

    last_one(c)
    for part in range(2):
        f_copy(last + 1 - c, part).wait_recv()
    last_one(1 - c)

    pl.when(home)(find_upper)

    def turn(t, _):
        cols = pl.ds(pl.multiple_of(t * 512, 512), 512)

        def block(j, _):
            rows = pl.ds(pl.multiple_of(j * TOK, TOK), TOK)
            feat_t[cols, rows] = feat[rows, cols].T
            return 0

        lax.fori_loop(0, 8, block, 0)
        return 0

    @pl.when(jnp.logical_not(home))
    def _():
        lax.fori_loop(0, 2, turn, 0)

    for i in (1, 2, 3, 0):
        to_y = lax.rem(y + i, 4)
        remote(
            stage.at[0, :, first], in_a1.at[to_y], a1_send.at[to_y], a1_recv.at[to_y], device_id=at(s, pair)
        ).wait_recv()
        total = keep_a[to_y] + in_a1[to_y].astype(F32)
        if i > 0:
            out_a2[to_y] = total.astype(BF16)
            post(a2_copy(to_y))
        else:
            own[:, 0:HALF] = total

    for step in range(2):
        z = 1 - zh if step == 0 else zh
        total = keep_b[z]
        for from_y in y_peers:
            slot = from_y * 2 + z
            remote(
                stage.at[0, :, second], in_b1.at[slot], b1_send.at[slot], b1_recv.at[slot],
                device_id=at(s, from_y * 2 + zh),
            ).wait_recv()
            total = total + in_b1[slot].astype(F32)
        if step == 0:
            out_b2[...] = total.astype(BF16)
            post(b2_copy())
        else:
            own[:, HALF:OUT] = total

    @pl.when(home)
    def _():
        lax.fori_loop(0, 2, turn, 0)

    lax.fori_loop(2, 3, turn, 0)

    inv_count = []
    for k in range(1, STEPS + 1):
        count = jnp.int32(0)
        for m in range(NMB):
            count = count + jnp.maximum(lengths[0, m] - k, 0)
        inv_count.append(1.0 / (jnp.full((1, 128), jnp.maximum(count, 1), jnp.int32).astype(F32) * D))

    here = pl.ds(pl.multiple_of(d * TOK, TOK), TOK)

    def draft(q, _):
        cols = pl.ds(pl.multiple_of(q * 128, 128), 128)
        joined = own[:, cols]
        up = upper[:, cols]
        dec = decay[:, cols]
        plen = left[...]

        def carry_of(k):
            return dec * mask_t[:, k - 1:k]

        state = joined
        pulls = []
        for k in range(1, STEPS + 1):
            state = joined + carry_of(k) * pltpu.roll(state, 1, 0)
            target = pltpu.roll(up, TOK - k, 0)
            diff = jnp.where(plen > k, state - target, 0.0)
            loss_acc[k - 1] += jnp.sum((diff * diff).reshape(TOK // 8, 8, 128), axis=0)
            pulls.append(diff * (2.0 * inv_count[k - 1]))
        back = pulls[STEPS - 1]
        total = back
        for k in range(STEPS - 1, 0, -1):
            back = pulls[k - 1] + pltpu.roll(carry_of(k + 1) * back, TOK - 1, 0)
            total = total + back
        total = total + pltpu.roll(carry_of(1) * back, TOK - 1, 0)
        rows_all[here, cols] = total.astype(BF16)
        return 0

    def rows_of(j):
        return pl.ds(pl.multiple_of(j * TOK, TOK), TOK)

    def q_copy(part, i, source, peer):
        block = rows_all.at[rows_of(source), first if part == 0 else second]
        return remote(block, block, q_send.at[part * 4 + i], q_recv.at[part * DP + source], device_id=at(s, peer))

    def qa_copy(i, from_y, to_y):
        block = rows_all.at[rows_of(from_y * 2 + 1 - zh), first]
        return remote(block, block, qa_send.at[i], qa_recv.at[from_y], device_id=at(s, to_y * 2 + zh))

    def qb_copy(i, from_y, z):
        block = rows_all.at[rows_of(from_y * 2 + z), second]
        return remote(block, block, qb_send.at[i], qb_recv.at[from_y], device_id=at(s, pair))

    early, sends[:] = list(sends), []
    b2_copy().wait_recv()
    own[:, HALF:OUT] += in_b2[...].astype(F32)
    lax.fori_loop(2, 4, draft, 0)
    over_y = [p * 2 + zh for p in y_peers]
    for i, peer in enumerate(over_y):
        post(q_copy(1, 1 + i, d, peer))
    for i, from_y in enumerate(y_peers):
        remote(
            out_a2.at[0], in_a2.at[from_y], a2_send.at[0], a2_recv.at[from_y], device_id=at(s, from_y * 2 + zh)
        ).wait_recv()
        own[:, 0:HALF] += in_a2[from_y].astype(F32)
    lax.fori_loop(0, 2, draft, 0)
    post(q_copy(0, 0, d, pair))
    lax.fori_loop(3, 4, turn, 0)
    for i, peer in enumerate(over_y):
        post(q_copy(0, 1 + i, d, peer))
    post(q_copy(1, 0, d, pair))
    q_copy(0, 0, pair, pair).wait_recv()
    for i, to_y in enumerate(y_peers):
        post(qa_copy(i, y, to_y))

    lax.fori_loop(4, 5, turn, 0)
    for i, from_y in enumerate(y_peers):
        q_copy(1, 0, from_y * 2 + zh, pair).wait_recv()
        post(qb_copy(i, from_y, zh))

    lane = lax.broadcasted_iota(jnp.int32, (8, 128), 1)
    losses = jnp.zeros((8, 128), F32)
    for k in range(1, STEPS + 1):
        losses = jnp.where(lane == k - 1, jnp.sum(loss_acc[k - 1]) * inv_count[k - 1], losses)
    loss_tile[...] = losses
    loss_all[s] = losses
    for i, peer in enumerate(seg_peers):
        post(remote(loss_tile, loss_all.at[s], l_send.at[i], l_recv.at[s], device_id=at(peer, d)))

    lax.fori_loop(5, 6, turn, 0)
    for copy in early:
        copy.wait_send()

    @pl.when(home)
    def _():
        for i in range(DP - 1):
            h_copy(i).wait_send()
            r2_copy(i).wait_send()

    for n in range(4):
        for part in range(2):
            f_copy(replica_of(c, n), part).wait_send()
    for to_y in range(4):
        a1_copy(to_y).wait_send()
    for to_y in y_peers:
        for z in range(2):
            b1_copy(to_y, z).wait_send()

    for i, peer in enumerate(seg_peers):
        remote(loss_tile, loss_all.at[peer], l_send.at[i], l_recv.at[peer], device_id=at(peer, d)).wait_recv()
    summed = loss_all[0]
    for i in range(1, SEG):
        summed = summed + loss_all[i]
    loss_out[...] = summed

    q_copy(1, 0, pair, pair).wait_recv()
    for from_y in y_peers:
        q_copy(0, 0, from_y * 2 + zh, pair).wait_recv()
        qa_copy(0, from_y, from_y).wait_recv()
        qb_copy(0, from_y, 1 - zh).wait_recv()

    for copy in sends:
        copy.wait_send()


def gradient(feat_t, rows, loss, grad_out, loss_out, grad, sem):
    def out_copy(t):
        return pltpu.make_async_copy(grad.at[t], grad_out.at[pl.ds(pl.multiple_of(t * CHUNK, CHUNK), CHUNK)], sem.at[t])

    def one(t, _):
        block = pl.ds(pl.multiple_of(t * CHUNK, CHUNK), CHUNK)
        grad[t] = jnp.dot(feat_t[block, :], rows[...], preferred_element_type=F32)
        out_copy(t).start()
        return 0

    lax.fori_loop(0, 3 * IN // CHUNK, one, 0)
    loss_out[...] = loss[0:1, 0:STEPS]
    for t in range(3 * IN // CHUNK):
        out_copy(t).wait()


def local(stream_in, sec_gain, sec_mix, fc_weight, decay, lengths, ttt_mask):
    vmem = pltpu.VMEM
    dma = pltpu.SemaphoreType.DMA
    scratch = [
        vmem((1, OUT), F32), pltpu.SMEM((1, NMB), jnp.int32), vmem((STEPS, TOK), jnp.int32),
        vmem((SECTIONS, 2, 1, D), F32),
        vmem((SECTIONS, 8, IN), F32), vmem((SECTIONS, 8, IN), F32),
        vmem((SECTIONS, 8, OUT), F32), vmem((SECTIONS, 8, OUT), F32),
        vmem((16, D), BF16), vmem((16, D), F32),
        vmem((4, TOK, IN), BF16),
        vmem((OWN, 128), F32), vmem((SEG, OWN, 128), F32),
        vmem((SECTIONS, 128), F32), vmem((DP, SECTIONS, 128), F32),
        vmem((TOK, 128), F32), vmem((SECTIONS, TOK, 128), F32),
        vmem((3 * IN, OUT), BF16),
        vmem((DP * TOK, 3 * IN), BF16),
        vmem((DP, TOK, OUT), BF16), vmem((4, TOK, HALF), F32), vmem((2, TOK, HALF), F32),
        vmem((4, TOK, HALF), BF16), vmem((DP, TOK, HALF), BF16),
        vmem((4, TOK, HALF), BF16), vmem((4, TOK, HALF), BF16),
        vmem((TOK, HALF), BF16), vmem((TOK, HALF), BF16), vmem((TOK, OUT), F32),
        vmem((TOK, OUT), BF16), vmem((TOK, OUT), F32),
        vmem((TOK, 128), F32), vmem((TOK, 128), F32), vmem((TOK, 128), jnp.int32),
        vmem((STEPS, 8, 128), F32), vmem((8, 128), F32), vmem((SEG, 8, 128), F32),
        dma((10,)), dma((5,)), dma((SEG,)), dma((10,)), dma((DP,)), dma((4,)),
        dma((SEG,)), dma((SEG,)), dma((DP,)), dma((DP,)), dma((DP,)), dma((DP,)),
        dma((4,)), dma((4,)), dma((DP,)), dma((DP,)), dma((4,)), dma((4,)), dma((1,)), dma((1,)),
        dma((8,)), dma((2 * DP,)), dma((3,)), dma((4,)), dma((3,)), dma((4,)), dma((SEG,)), dma((SEG,)),
    ]
    in_hbm = pl.BlockSpec(memory_space=pltpu.HBM)
    in_vmem = pl.BlockSpec(memory_space=pltpu.VMEM)
    loss, feat_t, rows = pl.pallas_call(
        kernel,
        out_shape=(
            vmem((8, 128), F32),
            vmem((3 * IN, DP * TOK), BF16),
            vmem((DP * TOK, OUT), BF16),
        ),
        in_specs=[in_hbm] * 7,
        out_specs=(in_vmem, in_vmem, in_vmem),
        scratch_shapes=scratch,
        compiler_params=pltpu.CompilerParams(
            collective_id=0, has_side_effects=True, vmem_limit_bytes=VM1 * 1024 * 1024
        ),
        name="window",
    )(stream_in, sec_gain, sec_mix, fc_weight, decay.reshape(1, OUT), lengths, ttt_mask)
    grad, step_loss = pl.pallas_call(
        gradient,
        out_shape=(
            jax.ShapeDtypeStruct((3 * IN, OUT), F32),
            jax.ShapeDtypeStruct((1, STEPS), F32),
        ),
        in_specs=[in_vmem] * 3,
        out_specs=(in_hbm, in_vmem),
        scratch_shapes=[vmem((3 * IN // CHUNK, CHUNK, OUT), F32), dma((3 * IN // CHUNK,))],
        compiler_params=pltpu.CompilerParams(vmem_limit_bytes=VM2 * 1024 * 1024),
        name="gradient",
    )(feat_t, rows, loss)
    return step_loss, grad.reshape(3, IN, OUT)


def solution(mesh):
    in_specs = (
        P("dp", None),
        P("segment", None),
        P("segment", None),
        P(None, "dp", "segment"),
        P("segment"),
        P("dp", None),
        P(None, "dp"),
    )
    out_specs = (P("dp", None), P(None, "dp", "segment"))
    return jax.shard_map(local, mesh=mesh, in_specs=in_specs, out_specs=out_specs, check_vma=False)
```

```python
import functools

import jax
import jax.numpy as jnp
from jax import lax
from jax.experimental import pallas as pl
from jax.experimental.pallas import tpu as pltpu
from jax.sharding import PartitionSpec as P

D = 8192
MB = 16
NMB = 8
STEPS = 7
SECTIONS = 16
TAPS = (0, SECTIONS // 2, SECTIONS - 1)
TOK = 128
SEG = 16
DP = 8
CHUNK = 1024
VM1 = 47
VM2 = 46
IN = D // DP
OUT = D // SEG
OWN = TOK // SEG
HALF = OUT // 2
F32 = jnp.float32
BF16 = jnp.bfloat16
MESH = pl.DeviceIdType.MESH


def at(segment, dp):
    return {"segment": segment, "dp": dp}


def advance(h, half_gain, mix, inv):
    u = (h * half_gain) * inv
    return (h + (mix * u) * (1.0 + jnp.tanh(u))).astype(BF16)


def run_sections(h, inv_of, gain_of, mix_of):
    rows, cols = h.shape
    taps = []
    for sec in range(SECTIONS):
        gain = jnp.concatenate([gain_of(sec)] * (rows // 8), 0)
        mix = jnp.concatenate([mix_of(sec)] * (rows // 8), 0)
        out = advance(h, gain, mix, jnp.concatenate([inv_of(sec)] * (cols // 128), 1))
        if sec in TAPS:
            taps.append(out)
        h = out.astype(F32)
    return taps


def kernel(stream, gain, mix, weight, decay_in, lengths_in, mask_in, loss_out, feat_t, rows_all,
           decay, lengths, mask, params, gain_b, mix_b, gain_u, mix_u, rows16, hx, h0, tile, sc1, packed, sc2, inv_own, inv_b,
           w, feat, stage, keep_a, keep_b, in_a1, in_b1, out_a2, in_a2, out_b2, in_b2, own,
           up_in, upper, mask_t, mask_pad, left, loss_acc, loss_tile, loss_all,
           in_sem, g_send, g_recv, gf_send, h_send, h_recv, r1_send, r1_recv, r2_send, r2_recv, f_send, f_recv,
           a1_send, a1_recv, b1_send, b1_recv, a2_send, a2_recv, b2_send, b2_recv,
           q_send, q_recv, qa_send, qa_recv, qb_send, qb_recv, l_send, l_recv):
    s = lax.axis_index("segment")
    d = lax.axis_index("dp")
    c = lax.rem(s, 2)
    y = d // 2
    zh = lax.rem(d, 2)
    pair = d + 1 - 2 * zh
    sib = s + 1 - 2 * c
    home = zh == c
    seg_peers = [lax.rem(s + i, SEG) for i in range(1, SEG)]
    y_peers = [lax.rem(y + i, 4) for i in range(1, 4)]
    plane = (s // 8) * 8
    x_peers = [plane + lax.rem(s - plane + 2 * i, 8) for i in range(1, 4)]
    across = lax.rem(s + 8, SEG)
    far = [(s, p * 2 + zh) for p in y_peers]
    far = [(across, lax.rem(y + i, 4) * 2 + 1 - zh) for i in (2, 1, 3, 0)] + far
    remote = functools.partial(pltpu.make_async_remote_copy, device_id_type=MESH)

    gain_copy = pltpu.make_async_copy(gain, params.at[s, 0], in_sem.at[5])
    mix_copy = pltpu.make_async_copy(mix, params.at[s, 1], in_sem.at[6])
    gain_copy.start()
    mix_copy.start()
    w_copies = [
        pltpu.make_async_copy(weight.at[i], w.at[pl.ds(i * IN, IN)], in_sem.at[i]) for i in range(3)
    ]
    row0 = pl.multiple_of((s // 2) * 16, 16)
    rows_copy = pltpu.make_async_copy(stream.at[pl.ds(row0, 16)], rows16, in_sem.at[3])
    up_copy = pltpu.make_async_copy(
        stream.at[:, pl.ds(pl.multiple_of(s * OUT, OUT), OUT)], up_in, in_sem.at[4]
    )
    small = [
        pltpu.make_async_copy(src, dst, in_sem.at[7 + i])
        for i, (src, dst) in enumerate(((decay_in, decay), (lengths_in, lengths), (mask_in, mask)))
    ]
    rows_copy.start()
    for copy in small:
        copy.start()

    barrier = pltpu.get_barrier_semaphore()
    for peer in [across, sib] + x_peers:
        pl.semaphore_signal(barrier, inc=1, device_id=at(peer, d), device_id_type=MESH)
    for seg, peer in far + [(s, pair)]:
        pl.semaphore_signal(barrier, inc=1, device_id=at(seg, peer), device_id_type=MESH)
    gain_copy.wait()
    params[s, 0] = 0.5 * params[s, 0]
    mix_copy.wait()
    pl.semaphore_wait(barrier, 5 + DP)

    def g_copy(slot, peer, send):
        return remote(params.at[slot], params.at[slot], send, g_recv.at[slot], device_id=at(peer, d))

    sends = []

    def post(copy):
        copy.start()
        sends.append(copy)

    for i, peer in enumerate([across] + x_peers + [sib]):
        post(g_copy(s, peer, g_send.at[i]))

    def h_copy(i):
        seg, peer = far[i]
        return remote(
            stream.at[:, pl.ds(pl.multiple_of(peer * IN, IN), IN)], h0.at[y],
            h_send.at[i], h_recv.at[y], device_id=at(seg, peer),
        )

    @pl.when(home)
    def _():
        for i in range(DP - 1):
            h_copy(i).start()
        pltpu.make_async_copy(
            stream.at[:, pl.ds(pl.multiple_of(d * IN, IN), IN)], h0.at[y], h_recv.at[y]
        ).start()

    up_copy.start()
    for copy in w_copies:
        copy.start()

    def wait_param(slot):
        g_copy(slot, sib, g_send.at[0]).wait_recv()

    wait_param(across)
    for i, peer in enumerate(x_peers + [sib]):
        post(g_copy(across, peer, gf_send.at[i]))

    for copy in small:
        copy.wait()
    token = lax.broadcasted_iota(jnp.int32, (TOK, 128), 0)
    pos = token & (MB - 1)
    micro = lax.shift_right_logical(token, 4)
    tok_len = jnp.zeros((TOK, 128), jnp.int32)
    for m in range(NMB):
        tok_len = jnp.where(micro == m, lengths[0, m], tok_len)
    left[...] = tok_len - pos
    mask_pad[...] = jnp.zeros_like(mask_pad)
    mask_pad[0:STEPS, :] = mask[...].astype(F32)
    mask_t[...] = jnp.where(pos >= 1, mask_pad[...].T, 0.0)
    loss_acc[...] = jnp.zeros_like(loss_acc)
    rows_copy.wait()
    hx[...] = rows16[...].astype(F32)

    for i, slot in enumerate(x_peers):
        wait_param(slot)
        post(g_copy(slot, sib, gf_send.at[4 + i]))
    for i, peer in enumerate(x_peers):
        slot = lax.rem(peer + 8, SEG)
        wait_param(slot)
        post(g_copy(slot, sib, gf_send.at[7 + i]))
    for i in range(SEG // 2):
        wait_param(lax.rem(sib + 2 * i, SEG))

    half = pl.ds(pl.multiple_of(c * OWN, OWN), OWN)
    lane = lax.broadcasted_iota(jnp.int32, (OWN, 128), 1)

    def inverse(h):
        return lax.rsqrt(jnp.sum(h * h, axis=1, keepdims=True) * (1.0 / D) + 1e-05)

    def scale_step(sec, carry):
        inv, acc = carry
        acc = jnp.where(lane == sec, inv, acc)
        h = advance(hx[half, :], params[sec, 0], params[sec, 1], inv).astype(F32)
        hx[half, :] = h
        return inverse(h), acc

    inv, acc = lax.fori_loop(
        0, SECTIONS - 1, scale_step, (inverse(hx[half, :]), jnp.zeros((OWN, 128), F32)), unroll=5
    )
    tile[...] = jnp.where(lane == SECTIONS - 1, inv, acc)
    sc1[s] = tile[...]
    chips = [lax.rem(s // 2 + i, SEG // 2) * 2 for i in (6, 2, 5, 7, 3, 1, 4)]
    for i, peer in enumerate([p + zh for p in chips] + [sib] + [p + 1 - zh for p in chips]):
        post(remote(tile, sc1.at[s], r1_send.at[i], r1_recv.at[s], device_id=at(peer, d)))

    def spread(sec, _):
        mine = pl.ds(pl.multiple_of(d * IN, IN), IN)
        loss_cols = pl.ds(pl.multiple_of(s * OUT, OUT), OUT)
        gain_b[sec] = jnp.broadcast_to(params[sec, 0, :, mine], (8, IN))
        mix_b[sec] = jnp.broadcast_to(params[sec, 1, :, mine], (8, IN))
        gain_u[sec] = jnp.broadcast_to(params[sec, 0, :, loss_cols], (8, OUT))
        mix_u[sec] = jnp.broadcast_to(params[sec, 1, :, loss_cols], (8, OUT))
        return 0

    lax.fori_loop(0, SECTIONS, spread, 0)
    for i, peer in enumerate(seg_peers):
        remote(tile, sc1.at[peer], r1_send.at[i], r1_recv.at[peer], device_id=at(peer, d)).wait_recv()
    inv_own[...] = sc1[...].reshape(TOK, 128)
    packed[...] = inv_own[...].T[0:SECTIONS, :]

    def r2_copy(i):
        seg, peer = far[i]
        return remote(packed, sc2.at[d], r2_send.at[i], r2_recv.at[d], device_id=at(seg, peer))

    @pl.when(home)
    def _():
        for i in range(DP - 1):
            r2_copy(i).start()
        sc2[d] = packed[...]

    up_copy.wait()

    def spread_rows(inv):
        for sec in range(SECTIONS):
            inv_b[sec] = jnp.broadcast_to(inv[:, sec:sec + 1], (TOK, 128))

    def find_upper():
        spread_rows(inv_own[...])

        def up_one(t, _):
            rows = pl.ds(pl.multiple_of(t * 32, 32), 32)
            taps = run_sections(
                up_in[rows, :].astype(F32), lambda sec: inv_b[sec, rows, :],
                lambda sec: gain_u[sec], lambda sec: mix_u[sec],
            )
            upper[rows, :] = taps[2].astype(F32)
            return 0

        lax.fori_loop(0, 4, up_one, 0)

    pl.when(jnp.logical_not(home))(find_upper)

    for copy in w_copies:
        copy.wait()

    first, second = pl.ds(0, HALF), pl.ds(HALF, HALF)

    def replica_of(parity, n):
        return lax.rem(y + n, 4) * 2 + parity

    def a1_copy(to_y):
        j = to_y * 2 + 1 - zh
        return remote(
            stage.at[j, :, first], in_a1.at[to_y], a1_send.at[to_y], a1_recv.at[to_y], device_id=at(s, pair)
        )

    def b1_copy(to_y, z):
        j = to_y * 2 + z
        return remote(
            stage.at[j, :, second], in_b1.at[y * 2 + z], b1_send.at[j], b1_recv.at[y * 2 + z],
            device_id=at(s, to_y * 2 + zh),
        )

    def a2_copy(to_y):
        return remote(
            out_a2.at[to_y], in_a2.at[y], a2_send.at[to_y], a2_recv.at[y], device_id=at(s, to_y * 2 + zh)
        )

    def b2_copy():
        return remote(out_b2, in_b2, b2_send.at[0], b2_recv.at[0], device_id=at(s, pair))

    def give(j, z, part):
        to_y = j // 2
        stage[j] = part.astype(BF16)

        @pl.when(z == zh)
        def _():
            keep_a[to_y] = part[:, 0:HALF]

        @pl.when(z != zh)
        def _():
            a1_copy(to_y).start()

        @pl.when(to_y == y)
        def _():
            keep_b[z] = part[:, HALF:OUT]

        @pl.when(to_y != y)
        def _():
            b1_copy(to_y, z).start()

    def f_copy(j, part):
        rows = pl.ds(pl.multiple_of(j * TOK + part * 64, 64), 64)
        slot = (j // 2) * 2 + part
        return remote(feat.at[rows], feat.at[rows], f_send.at[slot], f_recv.at[slot], device_id=at(sib, d))

    def join(n):
        to_y = lax.rem(y + n, 4)
        for part in range(2):
            f_copy(to_y * 2 + 1 - c, part).wait_recv()
        rows = pl.ds(pl.multiple_of(to_y * 2 * TOK, 2 * TOK), 2 * TOK)
        both = jnp.dot(feat[rows, :], w[...], preferred_element_type=F32)
        for z in range(2):
            give(to_y * 2 + z, z, both[z * TOK:(z + 1) * TOK, :])

    def work(n, _):
        j = replica_of(c, n)
        slot = j // 2
        remote(
            stream.at[:, pl.ds(0, IN)], h0.at[slot], h_send.at[0], h_recv.at[slot], device_id=at(sib, d)
        ).wait_recv()

        @pl.when(j != d)
        def _():
            remote(packed, sc2.at[j], r2_send.at[0], r2_recv.at[j], device_id=at(sib, d)).wait_recv()

        spread_rows(jnp.concatenate([sc2[j], jnp.zeros((128 - SECTIONS, 128), F32)], 0).T)

        def one(t, _):
            rows = pl.ds(pl.multiple_of(t * 16, 16), 16)
            taps = run_sections(
                h0[slot, rows, :].astype(F32), lambda sec: inv_b[sec, rows, :],
                lambda sec: gain_b[sec], lambda sec: mix_b[sec],
            )
            for i, tap in enumerate(taps):
                feat[pl.ds(pl.multiple_of(j * TOK + t * 16, 16), 16), i * IN:(i + 1) * IN] = tap
            return 0

        lax.fori_loop(0, 4, one, 0)
        f_copy(j, 0).start()
        lax.fori_loop(4, 8, one, 0)
        f_copy(j, 1).start()

        @pl.when(n > 0)
        def _():
            join(n - 1)

        return 0

    lax.fori_loop(0, 4, work, 0)

    last = lax.rem(y + 3, 4) * 2

    def last_one(z):
        j = last + z
        give(j, z, jnp.dot(feat[pl.ds(pl.multiple_of(j * TOK, TOK), TOK), :], w[...], preferred_element_type=F32))

    last_one(c)
    for part in range(2):
        f_copy(last + 1 - c, part).wait_recv()
    last_one(1 - c)

    pl.when(home)(find_upper)

    def turn(t, _):
        cols = pl.ds(pl.multiple_of(t * 512, 512), 512)

        def block(j, _):
            rows = pl.ds(pl.multiple_of(j * TOK, TOK), TOK)
            feat_t[cols, rows] = feat[rows, cols].T
            return 0

        lax.fori_loop(0, 8, block, 0)
        return 0

    @pl.when(jnp.logical_not(home))
    def _():
        lax.fori_loop(0, 2, turn, 0)

    for i in (1, 2, 3, 0):
        to_y = lax.rem(y + i, 4)
        remote(
            stage.at[0, :, first], in_a1.at[to_y], a1_send.at[to_y], a1_recv.at[to_y], device_id=at(s, pair)
        ).wait_recv()
        total = keep_a[to_y] + in_a1[to_y].astype(F32)
        if i > 0:
            out_a2[to_y] = total.astype(BF16)
            post(a2_copy(to_y))
        else:
            own[:, 0:HALF] = total

    for step in range(2):
        z = 1 - zh if step == 0 else zh
        total = keep_b[z]
        for from_y in y_peers:
            slot = from_y * 2 + z
            remote(
                stage.at[0, :, second], in_b1.at[slot], b1_send.at[slot], b1_recv.at[slot],
                device_id=at(s, from_y * 2 + zh),
            ).wait_recv()
            total = total + in_b1[slot].astype(F32)
        if step == 0:
            out_b2[...] = total.astype(BF16)
            post(b2_copy())
        else:
            own[:, HALF:OUT] = total

    @pl.when(home)
    def _():
        lax.fori_loop(0, 2, turn, 0)

    lax.fori_loop(2, 3, turn, 0)

    inv_count = []
    for k in range(1, STEPS + 1):
        count = jnp.int32(0)
        for m in range(NMB):
            count = count + jnp.maximum(lengths[0, m] - k, 0)
        inv_count.append(1.0 / (jnp.full((1, 128), jnp.maximum(count, 1), jnp.int32).astype(F32) * D))

    here = pl.ds(pl.multiple_of(d * TOK, TOK), TOK)

    def draft(q, _):
        cols = pl.ds(pl.multiple_of(q * 128, 128), 128)
        joined = own[:, cols]
        up = upper[:, cols]
        dec = decay[:, cols]
        plen = left[...]

        def carry_of(k):
            return dec * mask_t[:, k - 1:k]

        state = joined
        pulls = []
        for k in range(1, STEPS + 1):
            state = joined + carry_of(k) * pltpu.roll(state, 1, 0)
            target = pltpu.roll(up, TOK - k, 0)
            diff = jnp.where(plen > k, state - target, 0.0)
            loss_acc[k - 1] += jnp.sum((diff * diff).reshape(TOK // 8, 8, 128), axis=0)
            pulls.append(diff * (2.0 * inv_count[k - 1]))
        back = pulls[STEPS - 1]
        total = back
        for k in range(STEPS - 1, 0, -1):
            back = pulls[k - 1] + pltpu.roll(carry_of(k + 1) * back, TOK - 1, 0)
            total = total + back
        total = total + pltpu.roll(carry_of(1) * back, TOK - 1, 0)
        rows_all[here, cols] = total.astype(BF16)
        return 0

    def rows_of(j):
        return pl.ds(pl.multiple_of(j * TOK, TOK), TOK)

    def q_copy(part, i, source, peer):
        block = rows_all.at[rows_of(source), first if part == 0 else second]
        return remote(block, block, q_send.at[part * 4 + i], q_recv.at[part * DP + source], device_id=at(s, peer))

    def qa_copy(i, from_y, to_y):
        block = rows_all.at[rows_of(from_y * 2 + 1 - zh), first]
        return remote(block, block, qa_send.at[i], qa_recv.at[from_y], device_id=at(s, to_y * 2 + zh))

    def qb_copy(i, from_y, z):
        block = rows_all.at[rows_of(from_y * 2 + z), second]
        return remote(block, block, qb_send.at[i], qb_recv.at[from_y], device_id=at(s, pair))

    early, sends[:] = list(sends), []
    b2_copy().wait_recv()
    own[:, HALF:OUT] += in_b2[...].astype(F32)
    lax.fori_loop(2, 4, draft, 0)
    over_y = [p * 2 + zh for p in y_peers]
    for i, peer in enumerate(over_y):
        post(q_copy(1, 1 + i, d, peer))
    for i, from_y in enumerate(y_peers):
        remote(
            out_a2.at[0], in_a2.at[from_y], a2_send.at[0], a2_recv.at[from_y], device_id=at(s, from_y * 2 + zh)
        ).wait_recv()
        own[:, 0:HALF] += in_a2[from_y].astype(F32)
    lax.fori_loop(0, 2, draft, 0)
    post(q_copy(0, 0, d, pair))
    lax.fori_loop(3, 4, turn, 0)
    for i, peer in enumerate(over_y):
        post(q_copy(0, 1 + i, d, peer))
    post(q_copy(1, 0, d, pair))
    q_copy(0, 0, pair, pair).wait_recv()
    for i, to_y in enumerate(y_peers):
        post(qa_copy(i, y, to_y))

    lax.fori_loop(4, 5, turn, 0)
    for i, from_y in enumerate(y_peers):
        q_copy(1, 0, from_y * 2 + zh, pair).wait_recv()
        post(qb_copy(i, from_y, zh))

    lane = lax.broadcasted_iota(jnp.int32, (8, 128), 1)
    losses = jnp.zeros((8, 128), F32)
    for k in range(1, STEPS + 1):
        losses = jnp.where(lane == k - 1, jnp.sum(loss_acc[k - 1]) * inv_count[k - 1], losses)
    loss_tile[...] = losses
    loss_all[s] = losses
    for i, peer in enumerate(seg_peers):
        post(remote(loss_tile, loss_all.at[s], l_send.at[i], l_recv.at[s], device_id=at(peer, d)))

    lax.fori_loop(5, 6, turn, 0)
    for copy in early:
        copy.wait_send()

    @pl.when(home)
    def _():
        for i in range(DP - 1):
            h_copy(i).wait_send()
            r2_copy(i).wait_send()

    for n in range(4):
        for part in range(2):
            f_copy(replica_of(c, n), part).wait_send()
    for to_y in range(4):
        a1_copy(to_y).wait_send()
    for to_y in y_peers:
        for z in range(2):
            b1_copy(to_y, z).wait_send()

    for i, peer in enumerate(seg_peers):
        remote(loss_tile, loss_all.at[peer], l_send.at[i], l_recv.at[peer], device_id=at(peer, d)).wait_recv()
    summed = loss_all[0]
    for i in range(1, SEG):
        summed = summed + loss_all[i]
    loss_out[...] = summed

    q_copy(1, 0, pair, pair).wait_recv()
    for from_y in y_peers:
        q_copy(0, 0, from_y * 2 + zh, pair).wait_recv()
        qa_copy(0, from_y, from_y).wait_recv()
        qb_copy(0, from_y, 1 - zh).wait_recv()

    for copy in sends:
        copy.wait_send()


def gradient(feat_t, rows, loss, grad_out, loss_out, grad, sem):
    def out_copy(t):
        return pltpu.make_async_copy(grad.at[t], grad_out.at[pl.ds(pl.multiple_of(t * CHUNK, CHUNK), CHUNK)], sem.at[t])

    def one(t, _):
        block = pl.ds(pl.multiple_of(t * CHUNK, CHUNK), CHUNK)
        grad[t] = jnp.dot(feat_t[block, :], rows[...], preferred_element_type=F32)
        out_copy(t).start()
        return 0

    lax.fori_loop(0, 3 * IN // CHUNK, one, 0)
    loss_out[...] = loss[0:1, 0:STEPS]
    for t in range(3 * IN // CHUNK):
        out_copy(t).wait()


def local(stream_in, sec_gain, sec_mix, fc_weight, decay, lengths, ttt_mask):
    vmem = pltpu.VMEM
    dma = pltpu.SemaphoreType.DMA
    scratch = [
        vmem((1, OUT), F32), pltpu.SMEM((1, NMB), jnp.int32), vmem((STEPS, TOK), jnp.int32),
        vmem((SECTIONS, 2, 1, D), F32),
        vmem((SECTIONS, 8, IN), F32), vmem((SECTIONS, 8, IN), F32),
        vmem((SECTIONS, 8, OUT), F32), vmem((SECTIONS, 8, OUT), F32),
        vmem((16, D), BF16), vmem((16, D), F32),
        vmem((4, TOK, IN), BF16),
        vmem((OWN, 128), F32), vmem((SEG, OWN, 128), F32),
        vmem((SECTIONS, 128), F32), vmem((DP, SECTIONS, 128), F32),
        vmem((TOK, 128), F32), vmem((SECTIONS, TOK, 128), F32),
        vmem((3 * IN, OUT), BF16),
        vmem((DP * TOK, 3 * IN), BF16),
        vmem((DP, TOK, OUT), BF16), vmem((4, TOK, HALF), F32), vmem((2, TOK, HALF), F32),
        vmem((4, TOK, HALF), BF16), vmem((DP, TOK, HALF), BF16),
        vmem((4, TOK, HALF), BF16), vmem((4, TOK, HALF), BF16),
        vmem((TOK, HALF), BF16), vmem((TOK, HALF), BF16), vmem((TOK, OUT), F32),
        vmem((TOK, OUT), BF16), vmem((TOK, OUT), F32),
        vmem((TOK, 128), F32), vmem((TOK, 128), F32), vmem((TOK, 128), jnp.int32),
        vmem((STEPS, 8, 128), F32), vmem((8, 128), F32), vmem((SEG, 8, 128), F32),
        dma((10,)), dma((5,)), dma((SEG,)), dma((10,)), dma((DP,)), dma((4,)),
        dma((SEG,)), dma((SEG,)), dma((DP,)), dma((DP,)), dma((DP,)), dma((DP,)),
        dma((4,)), dma((4,)), dma((DP,)), dma((DP,)), dma((4,)), dma((4,)), dma((1,)), dma((1,)),
        dma((8,)), dma((2 * DP,)), dma((3,)), dma((4,)), dma((3,)), dma((4,)), dma((SEG,)), dma((SEG,)),
    ]
    in_hbm = pl.BlockSpec(memory_space=pltpu.HBM)
    in_vmem = pl.BlockSpec(memory_space=pltpu.VMEM)
    loss, feat_t, rows = pl.pallas_call(
        kernel,
        out_shape=(
            vmem((8, 128), F32),
            vmem((3 * IN, DP * TOK), BF16),
            vmem((DP * TOK, OUT), BF16),
        ),
        in_specs=[in_hbm] * 7,
        out_specs=(in_vmem, in_vmem, in_vmem),
        scratch_shapes=scratch,
        compiler_params=pltpu.CompilerParams(
            collective_id=0, has_side_effects=True, vmem_limit_bytes=VM1 * 1024 * 1024
        ),
        name="window",
    )(stream_in, sec_gain, sec_mix, fc_weight, decay.reshape(1, OUT), lengths, ttt_mask)
    grad, step_loss = pl.pallas_call(
        gradient,
        out_shape=(
            jax.ShapeDtypeStruct((3 * IN, OUT), F32),
            jax.ShapeDtypeStruct((1, STEPS), F32),
        ),
        in_specs=[in_vmem] * 3,
        out_specs=(in_hbm, in_vmem),
        scratch_shapes=[vmem((3 * IN // CHUNK, CHUNK, OUT), F32), dma((3 * IN // CHUNK,))],
        compiler_params=pltpu.CompilerParams(vmem_limit_bytes=VM2 * 1024 * 1024),
        name="gradient",
    )(feat_t, rows, loss)
    return step_loss, grad.reshape(3, IN, OUT)


def solution(mesh):
    in_specs = (
        P("dp", None),
        P("segment", None),
        P("segment", None),
        P(None, "dp", "segment"),
        P("segment"),
        P("dp", None),
        P(None, "dp"),
    )
    out_specs = (P("dp", None), P(None, "dp", "segment"))
    return jax.shard_map(local, mesh=mesh, in_specs=in_specs, out_specs=out_specs, check_vma=False)
```
